32 devices in a mesh: frame: 8 (over y, x, core), head: 4 (over z).
Axes of the slice: x: 2, y: 2, z: 4, core: 2. Of those that a mesh axis runs over, the one named last changes fastest.
Arguments:
- queries: bfloat16 [1792, 3072], P('frame', 'head'), may hold values from -24 to 24
- key_rows: bfloat16 [1792, 3072], P('frame', 'head'), may hold values from -24 to 24
- value_rows: bfloat16 [1792, 3072], P('frame', 'head'), may hold values from -5 to 5
- ref_keys: bfloat16 [8, 1024, 3072], P('frame', None, 'head'), may hold values from -5 to 5
- ref_values: bfloat16 [8, 1024, 3072], P('frame', None, 'head'), may hold values from -5 to 5
- key_lists: int32 [8, 8], P('frame'), may hold values from 0 to 7, as said below
- list_counts: int32 [8], P('frame'), may hold values from 1 to 7, as said below
- owner_index: int32 [1], replicated, may hold values from 0 to 7
- out_weight: bfloat16 [3072, 3072], P('head'), may hold values from -1.5 to 1.5
- residual: bfloat16 [1792, 3072], P('frame', 'head'), may hold values from -3 to 3
- gate_scale: float32 [3072], P('head'), may hold values from 0.5 to 2
Outputs:
- block_out: bfloat16 [1792, 3072], P('frame', 'head')
The draws below stay inside these ranges and needn't reach their ends.
Inputs may be any that keep to these rules, and one draw needn't show every extreme that they name: `key_lists`: the first list_counts[f] entries of row f are distinct frames other than f, each within 4 frames of f; the remaining entries equal f. `list_counts`: some frame lists every frame within 4 of it.
All inputs are finite; a program needn't handle non-finite values.
Results may differ from the reference program's by a relative error of at most 0.02.
Values may be sent and summed in bfloat16 or wider, within the bound.
No kernel may reach another device: no remote copies, remote signals or barrier semaphores. Data moves between devices by JAX's collectives and lax.ppermute only.
A program may use at most 64 MiB of HBM per device.

```python
import math
import jax
import jax.numpy as jnp
from jax import lax

D = 3072
HEADS = 24
HD = 128
TQ = 224
REF = 1024
REACH = 4
MAXL = 8
FRAMES = 8
TOKENS = 1792


def paired_rows(key):
    folded = jax.random.fold_in(key, 7)
    key_one, key_two = jax.random.split(folded)
    query_draw = jnp.clip(jax.random.normal(key_one, (TOKENS, D), jnp.float32), -4.0, 4.0)
    key_draw = jnp.clip(jax.random.normal(key_two, (TOKENS, D), jnp.float32), -4.0, 4.0)
    return (query_draw, key_draw)


def draw_queries(key, part):
    return paired_rows(key)[0].astype(jnp.bfloat16)


def draw_key_rows(key, part):
    return paired_rows(key)[1].astype(jnp.bfloat16)


def frame_lists(key):
    folded = jax.random.fold_in(key, 11)
    key_one, key_two, key_three = jax.random.split(folded, 3)
    frame_ids = jnp.arange(FRAMES, dtype=jnp.int32)[:, None]
    offsets = jnp.concatenate([jnp.arange(-REACH, 0, dtype=jnp.int32), jnp.arange(1, REACH + 1, dtype=jnp.int32)])
    candidates = frame_ids + offsets[None, :]
    inside = (candidates >= 0) & (candidates < FRAMES)
    available = jnp.sum(inside.astype(jnp.int32), axis=1)
    priority = jax.random.randint(key_one, (FRAMES, MAXL), 0, 1 << 20, dtype=jnp.int32) * MAXL + jnp.arange(MAXL, dtype=jnp.int32)[None, :]
    priority = jnp.where(inside, priority, -1)
    ranking = jnp.argsort(-priority, axis=1, stable=True)
    ordered = jnp.take_along_axis(candidates, ranking, axis=1)
    counts = jnp.minimum(jax.random.randint(key_two, (FRAMES,), 1, MAXL + 1, dtype=jnp.int32), available)
    full_frame = jnp.minimum(REACH + jax.random.randint(key_three, (), 0, max(FRAMES - 2 * REACH, 1), dtype=jnp.int32), FRAMES - 1)
    counts = jnp.where(frame_ids[:, 0] == full_frame, available, counts)
    slot_ids = jnp.arange(MAXL, dtype=jnp.int32)
    listed = jnp.where(slot_ids[None, :] < counts[:, None], ordered, frame_ids)
    return (listed.astype(jnp.int32), counts.astype(jnp.int32))


def draw_key_lists(key, part):
    return frame_lists(key)[0]


def draw_list_counts(key, part):
    return frame_lists(key)[1]


def block_levels(key, shape, cuts, low, high):
    loudness = 1.0
    for axis_at, blocks in cuts:
        steps = jax.random.uniform(jax.random.fold_in(jax.random.fold_in(key, 6), axis_at), (blocks,), jnp.float32, low / len(cuts), high / len(cuts))
        loudness = loudness * jnp.repeat(jnp.exp(steps), shape[axis_at] // blocks).reshape((-1,) + (1,) * (len(shape) - 1 - axis_at))
    return loudness


def centred(own_key, dims, scale, reach, cuts=(), kind=jnp.bfloat16):
    values = scale * jax.random.normal(own_key, dims, jnp.float32)
    if cuts:
        values = values * block_levels(own_key, dims, cuts, -0.22, 0.18)
    return jnp.clip(values, -reach, reach).astype(kind)


def setup_inputs(seed: int = 0) -> dict:
    splits = jax.random.split(jax.random.key(seed), 12)
    queries = draw_queries(jax.random.fold_in(splits[11], 71), 0)
    key_rows = draw_key_rows(jax.random.fold_in(splits[11], 71), 0)
    value_rows = centred(splits[2], (TOKENS, D), 1.0, 5.0, ((0, 8), (1, 4)))
    ref_keys = centred(splits[3], (FRAMES, REF, D), 1.0, 5.0, ((0, 8), (2, 4)))
    ref_values = centred(splits[4], (FRAMES, REF, D), 1.0, 5.0, ((0, 8), (2, 4)))
    key_lists = draw_key_lists(jax.random.fold_in(splits[11], 71), 0)
    list_counts = draw_list_counts(jax.random.fold_in(splits[11], 71), 0)
    owner_index = jax.random.randint(splits[7], (1,), 0, FRAMES).astype(jnp.int32)
    out_weight = centred(splits[8], (D, D), 0.25, 1.5, ((0, 4),))
    residual = centred(splits[9], (TOKENS, D), 0.5, 3.0, ((0, 8), (1, 4)))
    gate_scale = jnp.clip(jnp.exp(math.log(2.0) - 1.3862944 * jax.random.uniform(splits[10], (D,), jnp.float32) ** block_levels(splits[10], (D,), ((0, 4),), -0.2, 0.2)), 0.5, 2.0)
    return dict(queries=queries, key_rows=key_rows, value_rows=value_rows, ref_keys=ref_keys, ref_values=ref_values, key_lists=key_lists, list_counts=list_counts, owner_index=owner_index, out_weight=out_weight, residual=residual, gate_scale=gate_scale)


def reference(queries, key_rows, value_rows, ref_keys, ref_values, key_lists, list_counts, owner_index, out_weight, residual, gate_scale):
    inv_root = 1.0 / math.sqrt(HD)
    style_keys = lax.dynamic_index_in_dim(ref_keys, owner_index[0], 0, keepdims=False).astype(jnp.float32).reshape(REF, HEADS, HD)
    style_values = lax.dynamic_index_in_dim(ref_values, owner_index[0], 0, keepdims=False).astype(jnp.float32).reshape(REF, HEADS, HD)
    key_frames = key_rows.reshape(FRAMES, TQ, HEADS, HD)
    value_frames = value_rows.reshape(FRAMES, TQ, HEADS, HD)
    query_frames = queries.reshape(FRAMES, TQ, HEADS, HD)

    def attend_frame(frame_id):
        chosen = jnp.concatenate([frame_id[None].astype(jnp.int32), key_lists[frame_id].astype(jnp.int32)])
        slot_live = jnp.concatenate([jnp.ones((1,), bool), jnp.arange(MAXL, dtype=jnp.int32) < list_counts[frame_id]])
        near_keys = key_frames[chosen].astype(jnp.float32).reshape((MAXL + 1) * TQ, HEADS, HD)
        near_values = value_frames[chosen].astype(jnp.float32).reshape((MAXL + 1) * TQ, HEADS, HD)
        all_keys = jnp.concatenate([style_keys, near_keys], axis=0)
        all_values = jnp.concatenate([style_values, near_values], axis=0)
        allowed = jnp.concatenate([jnp.ones((REF,), bool), jnp.repeat(slot_live, TQ)])
        query_heads = query_frames[frame_id].astype(jnp.float32)
        scores = jnp.einsum('qhd,khd->hqk', query_heads, all_keys) * inv_root
        scores = jnp.where(allowed[None, None, :], scores, -jnp.inf)
        row_max = lax.optimization_barrier(jnp.max(scores, axis=-1, keepdims=True))
        weights = jnp.exp(scores - row_max)
        row_total = lax.optimization_barrier(jnp.sum(weights, axis=-1))
        rounded = lax.optimization_barrier(weights.astype(jnp.bfloat16)).astype(jnp.float32)
        combined = jnp.einsum('hqk,khd->qhd', rounded, all_values) / row_total.T[:, :, None]
        return combined.astype(jnp.bfloat16).reshape(TQ, D)
    attended = lax.map(attend_frame, jnp.arange(FRAMES, dtype=jnp.int32)).reshape(TOKENS, D)
    projected = jnp.dot(attended, out_weight, preferred_element_type=jnp.float32)
    return (residual.astype(jnp.float32) + gate_scale[None, :] * projected).astype(jnp.bfloat16)
```

```python
import functools
import math

import jax
import jax.numpy as jnp
from jax import lax
from jax.experimental import pallas as pl
from jax.experimental.pallas import tpu as pltpu
from jax.sharding import PartitionSpec as P

HD = 128
REACH = 4
LOG2E = 1.4426950408889634
VMEM_LIMIT = 48 * 1024 * 1024


def broadcast(block, axis, source):
    block = jnp.where(lax.axis_index(axis) == source, block, jnp.zeros_like(block))
    return lax.psum(block, axis)


def from_behind(block, axis, distance):
    devices = range(lax.axis_size(axis))
    route = [(i - distance, i) for i in devices if i - distance in devices]
    return lax.ppermute(block, axis, route)


def absorb(carried, query_heads, key_block, value_block, allowed):
    running_max, running_sum, weighted = carried
    head_count = query_heads.shape[1]
    key_heads = key_block.reshape(key_block.shape[0], head_count, HD)
    value_heads = value_block.reshape(value_block.shape[0], head_count, HD)
    scores = jnp.einsum(
        "qhd,khd->hqk", query_heads, key_heads, preferred_element_type=jnp.float32
    ) * (1.0 / math.sqrt(HD))
    if allowed is not None:
        scores = jnp.where(allowed[None, None, :], scores, -jnp.inf)
    new_max = jnp.maximum(running_max, jnp.max(scores, axis=-1))
    factor = jnp.exp(running_max - new_max)
    weights = jnp.exp(scores - new_max[:, :, None])
    running_sum = running_sum * factor + jnp.sum(weights, axis=-1)
    weighted = weighted * factor.T[:, :, None] + jnp.einsum(
        "hqk,khd->qhd",
        weights.astype(jnp.bfloat16),
        value_heads,
        preferred_element_type=jnp.float32,
    )
    return (new_max, running_sum, weighted)


def frame_block(carried, query_heads, key_block, value_block, begin_row, listed, live_slots):
    frame_of = (begin_row + jnp.arange(key_block.shape[0], dtype=jnp.int32)) // query_heads.shape[0]
    allowed = jnp.any((frame_of[:, None] == listed[None, :]) & live_slots[None, :], axis=1)
    return lax.cond(
        jnp.any(allowed),
        lambda current: absorb(current, query_heads, key_block, value_block, allowed),
        lambda current: current,
        carried,
    )


def general_device(
    queries,
    key_rows,
    value_rows,
    ref_keys,
    ref_values,
    key_lists,
    list_counts,
    owner_index,
    out_weight,
    residual,
    gate_scale,
):
    frame_len = queries.shape[0]
    columns_here = queries.shape[1]
    head_count = columns_here // HD
    query_heads = queries.reshape(frame_len, head_count, HD)
    listed = key_lists[0]
    live_slots = jnp.arange(listed.shape[0], dtype=jnp.int32) < list_counts[0]
    position = lax.axis_index("frame")
    carried = (
        jnp.full((head_count, frame_len), -jnp.inf, jnp.float32),
        jnp.zeros((head_count, frame_len), jnp.float32),
        jnp.zeros((frame_len, head_count, HD), jnp.float32),
    )
    style_keys, style_values = (
        broadcast(ref_keys, "frame", owner_index[0]),
        broadcast(ref_values, "frame", owner_index[0]),
    )
    carried = absorb(carried, query_heads, style_keys[0], style_values[0], None)
    carried = absorb(carried, query_heads, key_rows, value_rows, None)
    for offset in list(range(1, REACH + 1)) + list(range(-REACH, 0)):
        moved_keys, moved_values = from_behind((key_rows, value_rows), "frame", offset)
        carried = frame_block(
            carried,
            query_heads,
            moved_keys,
            moved_values,
            (position - offset) * frame_len,
            listed,
            live_slots,
        )
    running_max, running_sum, weighted = carried
    attended = (
        (weighted / running_sum.T[:, :, None]).astype(jnp.bfloat16).reshape(frame_len, columns_here)
    )
    shares = lax.psum_scatter(
        lax.dot_general(
            out_weight, attended, (((0,), (1,)), ((), ())), preferred_element_type=jnp.float32
        ).astype(jnp.bfloat16),
        "head",
        scatter_dimension=0,
        tiled=True,
    ).astype(jnp.float32)
    return (residual.astype(jnp.float32) + gate_scale[None, :] * shares.T).astype(jnp.bfloat16)


CORE, ROW, COLUMN = 1, 2, 4
PAD = 256
SLOTS = (0, 2, 4, 6, 1, 3, 5, 7)


def swap(block, axis, bit):
    return lax.ppermute(block, axis, [(i, i ^ bit) for i in range(lax.axis_size(axis))])


def halves(width):
    x = (lax.axis_index("frame") // ROW) % 2
    mine = pl.multiple_of(x * width, HD)
    other = pl.multiple_of((1 - x) * width, HD)
    return mine, other


def visible(frame, lists, counts):
    seen = frame == lax.axis_index("frame")
    for j in range(lists.shape[1]):
        seen = seen | ((lists[0, j] == frame) & (j < counts[0]))
    return seen


def split_kernel(lists, counts, q, k, v, kv_keep, kv_send, q_keep, q_send):
    rows, width = q_keep.shape
    mine, other = halves(width)
    kv_send[:rows, :] = k[:, pl.ds(other, width)]
    kv_send[rows:, :] = v[:, pl.ds(other, width)]
    kv_keep[:rows, :] = k[:, pl.ds(mine, width)]
    kv_keep[rows:, :] = v[:, pl.ds(mine, width)]
    q_keep[...] = q[:, pl.ds(mine, width)]
    q_send[:rows, :] = q[:, pl.ds(other, width)]
    lane = lax.broadcasted_iota(jnp.int32, (16, width), 1)
    flags = jnp.zeros((16, width), jnp.float32)
    for g in range(lax.axis_size("frame")):
        flag = jnp.where(visible(g, lists, counts), 1.0, 0.0)
        flags = jnp.where(lane == g, flag, flags)
    q_send[rows:, :] = flags.astype(jnp.bfloat16)


def pick_kernel(owner, k, v, from_even, from_odd, send_a, send_b, keep, sems):
    chunk, width = send_a.shape
    mine, other = halves(width)
    core = lax.axis_index("frame") % 2
    owner_core = owner[0] % 2

    def take(src):
        copies = [
            pltpu.make_async_copy(
                src.at[0, pl.ds(0, chunk), pl.ds(other, width)], send_a, sems.at[0]
            ),
            pltpu.make_async_copy(
                src.at[0, pl.ds(chunk, chunk), pl.ds(other, width)], send_b, sems.at[1]
            ),
            pltpu.make_async_copy(src.at[0, :, pl.ds(mine, width)], keep, sems.at[2]),
        ]
        for copy in copies:
            copy.start()
        for copy in copies:
            copy.wait()

    for at, here, there in ((0, k, from_odd), (1, v, from_even)):
        pl.when((core == at) & (owner_core == at))(functools.partial(take, here))
        pl.when((core == at) & (owner_core != at))(functools.partial(take, there))


NT = (((1,), (1,)), ((), ()))
TN = (((0,), (0,)), ((), ()))


def absorb_chunk(query, keys, values, biases, state):
    scale = LOG2E / math.sqrt(HD)
    scores = [lax.dot_general(k, query, NT, preferred_element_type=jnp.float32) for k in keys]
    top = None
    for s, b in zip(scores, biases):
        t = jnp.max(s, axis=0, keepdims=True) * scale
        t = t if b is None else t + b
        top = t if top is None else jnp.maximum(top, t)
    if state is not None:
        old_top, old_sum, old_acc = state
        top = jnp.maximum(old_top, top)
    total, acc = None, None
    for s, b, v in zip(scores, biases, values):
        shift = top if b is None else top - b
        p = jnp.exp2(s * scale - shift)
        part = jnp.sum(p, axis=0, keepdims=True)
        total = part if total is None else total + part
        o = lax.dot_general(v, p.astype(jnp.bfloat16), TN, preferred_element_type=jnp.float32)
        acc = o if acc is None else acc + o
    if state is not None:
        factor = jnp.exp2(old_top - top)
        total = total + old_sum * factor
        acc = acc + old_acc * factor
    return top, total, acc


def frames_kernel(lists, counts, q_keep, q_got, *rest):
    kv = rest[: len(SLOTS)]
    acc_out, stat_out, q_pad = rest[len(SLOTS) :]
    rows, width = q_keep.shape
    heads = width // HD
    here = lax.axis_index("frame")
    q_pad[...] = jnp.zeros_like(q_pad)
    q_pad[:rows, :] = q_keep[...]
    q_pad[PAD : PAD + rows, :] = q_got[:rows, :]
    flags = q_got[rows : rows + 16, :].astype(jnp.float32)
    lane = lax.broadcasted_iota(jnp.int32, (16, width), 1)
    side = lax.broadcasted_iota(jnp.int32, (1, 2 * PAD), 1)
    biases = []
    for bit in SLOTS:
        frame = here ^ bit
        own = jnp.where(visible(frame, lists, counts), 0.0, -jnp.inf)
        seen = jnp.max(jnp.where(lane == frame, flags, 0.0), keepdims=True)
        theirs = jnp.where(seen > 0.5, 0.0, -jnp.inf)
        biases.append(jnp.where(side < PAD, own, theirs))
    stat_out[...] = jnp.zeros_like(stat_out)
    for h in range(heads):
        cols = slice(h * HD, (h + 1) * HD)
        query = q_pad[:, cols]
        state = None
        for s in range(0, len(SLOTS), 2):
            state = absorb_chunk(
                query,
                [kv[s][:rows, cols], kv[s + 1][:rows, cols]],
                [kv[s][rows:, cols], kv[s + 1][rows:, cols]],
                biases[s : s + 2],
                state,
            )
        top, total, acc = state
        stat_out[h : h + 1, :] = top
        stat_out[heads + h : heads + h + 1, :] = total
        acc_out[cols, :] = acc


def style_kernel(last, q_pad, held, swapped, acc_in, stat_in, *rest):
    outs, (keys, values) = rest[:2], rest[2:]
    chunk, width = keys.shape
    heads = width // HD
    core = lax.axis_index("frame") % 2

    @pl.when(core == 0)
    def _():
        keys[...] = held[...]
        values[...] = swapped[...]

    @pl.when(core == 1)
    def _():
        keys[...] = swapped[...]
        values[...] = held[...]

    if not last:
        acc_out, stat_out = outs
        stat_out[...] = jnp.zeros_like(stat_out)
    for h in range(heads):
        cols = slice(h * HD, (h + 1) * HD)
        state = (stat_in[h : h + 1, :], stat_in[heads + h : heads + h + 1, :], acc_in[cols, :])
        top, total, acc = absorb_chunk(
            q_pad[:, cols], [keys[:, cols]], [values[:, cols]], [None], state
        )
        if last:
            own, theirs = outs
            rows = own.shape[0]
            done = (acc / total).T.astype(jnp.bfloat16)
            own[:, cols] = done[:rows, :]
            theirs[:, cols] = done[PAD : PAD + rows, :]
        else:
            stat_out[h : h + 1, :] = top
            stat_out[heads + h : heads + h + 1, :] = total
            acc_out[cols, :] = acc


def project_kernel(order, own, got, weight, *rest):
    outs, (blocks, sems) = rest[: len(order)], rest[len(order) :]
    width = own.shape[1]
    columns = outs[0].shape[1]
    mine, other = halves(width)
    place = lax.axis_index("head")
    copies = []
    for i, bit in enumerate(order):
        start = pl.multiple_of((place ^ bit) * columns, HD)
        copies.append(
            pltpu.make_async_copy(weight.at[:, pl.ds(start, columns)], blocks.at[i], sems.at[i])
        )
        copies[-1].start()
    for i, out in enumerate(outs):
        copies[i].wait()
        share = jnp.dot(
            own[...], blocks[i, pl.ds(mine, width), :], preferred_element_type=jnp.float32
        ) + jnp.dot(got[...], blocks[i, pl.ds(other, width), :], preferred_element_type=jnp.float32)
        out[...] = share.astype(out.dtype)


SMEM = pl.BlockSpec(memory_space=pltpu.SMEM)
VMEM = pl.BlockSpec(memory_space=pltpu.VMEM)
ANY = pl.BlockSpec(memory_space=pl.ANY)


def call(kernel, in_specs, outs, scratch=(), out_spec=VMEM, flops=0, moved=0, exps=0):
    shapes = [jax.ShapeDtypeStruct(shape, dtype) for shape, dtype in outs]
    return pl.pallas_call(
        kernel,
        out_shape=shapes,
        in_specs=in_specs,
        out_specs=[out_spec] * len(shapes),
        scratch_shapes=list(scratch),
        compiler_params=pltpu.CompilerParams(vmem_limit_bytes=VMEM_LIMIT),
        cost_estimate=pl.CostEstimate(flops=flops, bytes_accessed=moved, transcendentals=exps),
    )


def paired_device(
    queries,
    key_rows,
    value_rows,
    ref_keys,
    ref_values,
    key_lists,
    list_counts,
    owner_index,
    out_weight,
    residual,
    gate_scale,
):
    bf16, f32 = jnp.bfloat16, jnp.float32
    rows, columns = queries.shape
    width = columns // 2
    heads = width // HD
    style = ref_keys.shape[1]
    chunk = style // 2
    frames, planes = lax.axis_size("frame"), lax.axis_size("head")
    owner = owner_index[0]
    here = lax.axis_index("frame")

    even = [(i, i ^ CORE) for i in range(0, frames, 2)]
    odd = [(i ^ CORE, i) for i in range(0, frames, 2)]
    from_even = lax.ppermute(ref_values, "frame", even)
    from_odd = lax.ppermute(ref_keys, "frame", odd)

    kv = (2 * rows, width)
    kv_keep, kv_send, q_keep, q_send = call(
        split_kernel,
        [SMEM, SMEM, VMEM, VMEM, VMEM],
        [(kv, bf16), (kv, bf16), ((rows, width), bf16), ((rows + 16, width), bf16)],
        moved=12 * rows * columns,
    )(key_lists, list_counts, queries, key_rows, value_rows)

    kv_x = swap(kv_send, "frame", ROW)
    kv_y = swap(kv_keep, "frame", COLUMN)
    kv_xy = swap(kv_x, "frame", COLUMN)

    part = (chunk, width)
    send_a, send_b, keep = call(
        pick_kernel,
        [SMEM, ANY, ANY, ANY, ANY],
        [(part, bf16), (part, bf16), ((style, width), bf16)],
        scratch=[pltpu.SemaphoreType.DMA((3,))],
        out_spec=ANY,
        moved=4 * style * columns,
    )(owner_index, ref_keys, ref_values, from_even, from_odd)

    same_x = (owner // ROW) % 2 == (here // ROW) % 2
    same_y = (owner // COLUMN) % 2 == (here // COLUMN) % 2
    held = []
    for j, sent in enumerate((send_a, send_b)):
        came = swap(sent, "frame", ROW)
        chosen = jnp.where(same_x, keep[j * chunk : (j + 1) * chunk], came)
        came = swap(chosen, "frame", COLUMN)
        held.append(jnp.where(same_y, chosen, came))
    q_got = swap(q_send, "frame", ROW)

    near = [kv_keep, kv_x, kv_y, kv_xy]
    near = near + [swap(block, "frame", CORE) for block in near]
    state = [((width, 2 * PAD), f32), ((8, 2 * PAD), f32)]
    pairs = 2 * PAD * width
    acc, stats, q_pad = call(
        frames_kernel,
        [SMEM, SMEM] + [VMEM] * 10,
        state + [((2 * PAD, width), bf16)],
        flops=4 * pairs * 8 * rows,
        exps=2 * PAD * heads * 8 * rows,
        moved=16 * rows * width * 2,
    )(key_lists, list_counts, q_keep, q_got, *near)

    scratch = [pltpu.VMEM(part, bf16), pltpu.VMEM(part, bf16)]
    cost = dict(flops=4 * pairs * chunk, exps=2 * PAD * heads * chunk, moved=8 * chunk * width)
    acc, stats = call(
        functools.partial(style_kernel, False), [VMEM] * 5, state, scratch=scratch, **cost
    )(q_pad, held[0], swap(held[0], "frame", CORE), acc, stats)
    own, theirs = call(
        functools.partial(style_kernel, True),
        [VMEM] * 5,
        [((rows, width), bf16)] * 2,
        scratch=scratch,
        **cost,
    )(q_pad, held[1], swap(held[1], "frame", CORE), acc, stats)
    got = swap(theirs, "frame", ROW)

    order = sorted(range(1, planes), key=lambda bit: bit == 1) + [0]
    shares = call(
        functools.partial(project_kernel, order),
        [VMEM, VMEM, ANY],
        [((rows, columns), bf16)] * (planes - 1) + [((rows, columns), f32)],
        scratch=[
            pltpu.VMEM((planes, columns, columns), bf16),
            pltpu.SemaphoreType.DMA((planes,)),
        ],
        flops=2 * rows * columns * columns * planes,
        moved=2 * columns * columns * planes,
    )(own, got, out_weight)
    projected = shares[-1]
    for bit, share in zip(order, shares[:-1]):
        projected = projected + swap(share, "head", bit).astype(f32)
    return (residual.astype(f32) + gate_scale[None, :] * projected).astype(bf16)


def solution(mesh):
    placed = (
        P("frame", "head"),
        P("frame", "head"),
        P("frame", "head"),
        P("frame", None, "head"),
        P("frame", None, "head"),
        P("frame", None),
        P("frame"),
        P(),
        P("head", None),
        P("frame", "head"),
        P("head"),
    )

    def per_device(*args):
        rows, columns = args[0].shape
        style = args[3].shape[1]
        planes = mesh.shape["head"]
        paired = (
            mesh.shape["frame"] == 8
            and planes & (planes - 1) == 0
            and columns % (2 * HD) == 0
            and columns // HD <= 8
            and rows % 16 == 0
            and rows <= PAD
            and style % 32 == 0
        )
        return (paired_device if paired else general_device)(*args)

    return jax.shard_map(
        per_device, mesh=mesh, in_specs=placed, out_specs=P("frame", "head"), check_vma=False
    )
```

```python
import functools
import math

import jax
import jax.numpy as jnp
from jax import lax
from jax.experimental import pallas as pl
from jax.experimental.pallas import tpu as pltpu
from jax.sharding import PartitionSpec as P

HD = 128
REACH = 4
LOG2E = 1.4426950408889634
VMEM_LIMIT = 24 * 1024 * 1024


def broadcast(block, axis, source):
    block = jnp.where(lax.axis_index(axis) == source, block, jnp.zeros_like(block))
    return lax.psum(block, axis)


def from_behind(block, axis, distance):
    devices = range(lax.axis_size(axis))
    route = [(i - distance, i) for i in devices if i - distance in devices]
    return lax.ppermute(block, axis, route)


def absorb(carried, query_heads, key_block, value_block, allowed):
    running_max, running_sum, weighted = carried
    head_count = query_heads.shape[1]
    key_heads = key_block.reshape(key_block.shape[0], head_count, HD)
    value_heads = value_block.reshape(value_block.shape[0], head_count, HD)
    scores = jnp.einsum(
        "qhd,khd->hqk", query_heads, key_heads, preferred_element_type=jnp.float32
    ) * (1.0 / math.sqrt(HD))
    if allowed is not None:
        scores = jnp.where(allowed[None, None, :], scores, -jnp.inf)
    new_max = jnp.maximum(running_max, jnp.max(scores, axis=-1))
    factor = jnp.exp(running_max - new_max)
    weights = jnp.exp(scores - new_max[:, :, None])
    running_sum = running_sum * factor + jnp.sum(weights, axis=-1)
    weighted = weighted * factor.T[:, :, None] + jnp.einsum(
        "hqk,khd->qhd",
        weights.astype(jnp.bfloat16),
        value_heads,
        preferred_element_type=jnp.float32,
    )
    return (new_max, running_sum, weighted)


def frame_block(carried, query_heads, key_block, value_block, begin_row, listed, live_slots):
    frame_of = (begin_row + jnp.arange(key_block.shape[0], dtype=jnp.int32)) // query_heads.shape[0]
    allowed = jnp.any((frame_of[:, None] == listed[None, :]) & live_slots[None, :], axis=1)
    return lax.cond(
        jnp.any(allowed),
        lambda current: absorb(current, query_heads, key_block, value_block, allowed),
        lambda current: current,
        carried,
    )


def general_device(
    queries,
    key_rows,
    value_rows,
    ref_keys,
    ref_values,
    key_lists,
    list_counts,
    owner_index,
    out_weight,
    residual,
    gate_scale,
):
    frame_len = queries.shape[0]
    columns_here = queries.shape[1]
    head_count = columns_here // HD
    query_heads = queries.reshape(frame_len, head_count, HD)
    listed = key_lists[0]
    live_slots = jnp.arange(listed.shape[0], dtype=jnp.int32) < list_counts[0]
    position = lax.axis_index("frame")
    carried = (
        jnp.full((head_count, frame_len), -jnp.inf, jnp.float32),
        jnp.zeros((head_count, frame_len), jnp.float32),
        jnp.zeros((frame_len, head_count, HD), jnp.float32),
    )
    style_keys, style_values = (
        broadcast(ref_keys, "frame", owner_index[0]),
        broadcast(ref_values, "frame", owner_index[0]),
    )
    carried = absorb(carried, query_heads, style_keys[0], style_values[0], None)
    carried = absorb(carried, query_heads, key_rows, value_rows, None)
    for offset in list(range(1, REACH + 1)) + list(range(-REACH, 0)):
        moved_keys, moved_values = from_behind((key_rows, value_rows), "frame", offset)
        carried = frame_block(
            carried,
            query_heads,
            moved_keys,
            moved_values,
            (position - offset) * frame_len,
            listed,
            live_slots,
        )
    running_max, running_sum, weighted = carried
    attended = (
        (weighted / running_sum.T[:, :, None]).astype(jnp.bfloat16).reshape(frame_len, columns_here)
    )
    shares = lax.psum_scatter(
        lax.dot_general(
            out_weight, attended, (((0,), (1,)), ((), ())), preferred_element_type=jnp.float32
        ).astype(jnp.bfloat16),
        "head",
        scatter_dimension=0,
        tiled=True,
    ).astype(jnp.float32)
    return (residual.astype(jnp.float32) + gate_scale[None, :] * shares.T).astype(jnp.bfloat16)


CORE, ROW, COLUMN = 1, 2, 4
PAD = 256
SLOTS = (0, 2, 4, 6, 1, 3, 5, 7)


def swap(block, axis, bit, name):
    with jax.named_scope(name):
        return lax.ppermute(block, axis, [(i, i ^ bit) for i in range(lax.axis_size(axis))])


def halves(width):
    x = (lax.axis_index("frame") // ROW) % 2
    mine = pl.multiple_of(x * width, HD)
    other = pl.multiple_of((1 - x) * width, HD)
    return mine, other


def visible(frame, lists, counts):
    seen = frame == lax.axis_index("frame")
    for j in range(lists.shape[1]):
        seen = seen | ((lists[0, j] == frame) & (j < counts[0]))
    return seen


def split_kernel(k, v, keep, send, sems):
    rows, width = keep.shape[0], keep.shape[1] // 2
    mine, other = halves(width)
    left, right = pl.ds(0, width), pl.ds(width, width)
    move(
        sems,
        (k.at[:, pl.ds(other, width)], send.at[:, left]),
        (v.at[:, pl.ds(other, width)], send.at[:, right]),
        (k.at[:, pl.ds(mine, width)], keep.at[:, left]),
        (v.at[:, pl.ds(mine, width)], keep.at[:, right]),
    )


def query_kernel(lists, counts, q, after, keep, send, sems):
    rows, width = keep.shape
    mine, other = halves(width)
    lane = lax.broadcasted_iota(jnp.int32, (16, width), 1)
    flags = jnp.zeros((16, width), jnp.float32)
    for g in range(lax.axis_size("frame")):
        flag = jnp.where(visible(g, lists, counts), 1.0, 0.0)
        flags = jnp.where(lane == g, flag, flags)
    send[rows:, :] = flags.astype(jnp.bfloat16)
    move(
        sems,
        (q.at[:, pl.ds(mine, width)], keep),
        (q.at[:, pl.ds(other, width)], send.at[pl.ds(0, rows)]),
    )


def from_owner(owner, k, v, from_even, from_odd, take):
    core = lax.axis_index("frame") % 2
    owner_core = owner[0] % 2
    for at, here, there in ((0, k, from_odd), (1, v, from_even)):
        pl.when((core == at) & (owner_core == at))(functools.partial(take, here))
        pl.when((core == at) & (owner_core != at))(functools.partial(take, there))


def move(sems, *pairs):
    copies = [pltpu.make_async_copy(src, dst, sems.at[i]) for i, (src, dst) in enumerate(pairs)]
    for copy in copies:
        copy.start()
    for copy in copies:
        copy.wait()


def pick_kernel(owner, k, v, from_even, from_odd, send_a, send_b, keep, sems):
    first, width = send_a.shape
    second = send_b.shape[0]
    mine, other = halves(width)

    def take(src):
        move(
            sems,
            (src.at[0, pl.ds(0, first), pl.ds(other, width)], send_a),
            (src.at[0, pl.ds(first, second), pl.ds(other, width)], send_b),
            (src.at[0, :, pl.ds(mine, width)], keep),
        )

    from_owner(owner, k, v, from_even, from_odd, take)


def after_kernel(*refs):
    pass


def choose_kernel(bit, begin, owner, here, came, *rest):
    out, sems = rest[-2:]
    own = (owner[0] // bit) % 2 == (lax.axis_index("frame") // bit) % 2

    @pl.when(own)
    def _():
        move(sems, (here.at[pl.ds(begin, out.shape[0])], out))

    @pl.when(jnp.logical_not(own))
    def _():
        move(sems, (came, out))


NT = (((1,), (1,)), ((), ()))
TN = (((0,), (0,)), ((), ()))


def absorb_chunk(query, keys, values, biases, state):
    scale = LOG2E / math.sqrt(HD)
    scores = [lax.dot_general(k, query, NT, preferred_element_type=jnp.float32) for k in keys]
    top = None
    for s, b in zip(scores, biases):
        t = jnp.max(s, axis=0, keepdims=True) * scale
        t = t if b is None else t + b
        top = t if top is None else jnp.maximum(top, t)
    if state is not None:
        old_top, old_sum, old_acc = state
        top = jnp.maximum(old_top, top)
    total, acc = None, None
    for s, b, v in zip(scores, biases, values):
        shift = top if b is None else top - b
        p = jnp.exp2(s * scale - shift)
        part = jnp.sum(p, axis=0, keepdims=True)
        total = part if total is None else total + part
        o = lax.dot_general(v, p.astype(jnp.bfloat16), TN, preferred_element_type=jnp.float32)
        acc = o if acc is None else acc + o
    if state is not None:
        factor = jnp.exp2(old_top - top)
        total = total + old_sum * factor
        acc = acc + old_acc * factor
    return top, total, acc


def frames_kernel(remote, lists, counts, q, *rest):
    kv = rest[: len(SLOTS)]
    acc_out, stat_out, padded = rest[len(SLOTS) :]
    rows, width = kv[0].shape[0], kv[0].shape[1] // 2
    heads = width // HD
    here = lax.axis_index("frame")
    padded[...] = jnp.zeros_like(padded)
    padded[:rows, :] = q[:rows, :]
    if remote:
        flags = q[rows : rows + 16, :].astype(jnp.float32)
        lane = lax.broadcasted_iota(jnp.int32, (16, width), 1)
    biases = []
    for bit in SLOTS:
        frame = here ^ bit
        if remote:
            seen = jnp.max(jnp.where(lane == frame, flags, 0.0), keepdims=True)
            bias = jnp.where(seen > 0.5, 0.0, -jnp.inf)
        else:
            bias = jnp.where(visible(frame, lists, counts), 0.0, -jnp.inf)
        biases.append(jnp.broadcast_to(bias, (1, PAD)))
    stat_out[...] = jnp.zeros_like(stat_out)
    for h in range(heads):
        keys = slice(h * HD, (h + 1) * HD)
        values = slice(width + h * HD, width + (h + 1) * HD)
        state = None
        for s in range(0, len(SLOTS), 2):
            pair = kv[s : s + 2]
            state = absorb_chunk(
                padded[:, keys],
                [block[:, keys] for block in pair],
                [block[:, values] for block in pair],
                biases[s : s + 2],
                state,
            )
        top, total, acc = state
        stat_out[h : h + 1, :] = top
        stat_out[heads + h : heads + h + 1, :] = total
        acc_out[keys, :] = acc


def style_kernel(last, rows, q, held, swapped, acc_in, stat_in, *rest):
    outs, (keys, values, padded) = rest[:-3], rest[-3:]
    chunk, width = keys.shape
    heads = width // HD
    core = lax.axis_index("frame") % 2
    padded[...] = jnp.zeros_like(padded)
    padded[:rows, :] = q[:rows, :]

    @pl.when(core == 0)
    def _():
        keys[...] = held[...]
        values[...] = swapped[...]

    @pl.when(core == 1)
    def _():
        keys[...] = swapped[...]
        values[...] = held[...]

    if not last:
        acc_out, stat_out = outs
        stat_out[...] = jnp.zeros_like(stat_out)
    for h in range(heads):
        cols = slice(h * HD, (h + 1) * HD)
        state = (stat_in[h : h + 1, :], stat_in[heads + h : heads + h + 1, :], acc_in[cols, :])
        top, total, acc = absorb_chunk(
            padded[:, cols], [keys[:, cols]], [values[:, cols]], [None], state
        )
        if last:
            outs[0][:, cols] = (acc / total).T.astype(jnp.bfloat16)[:rows, :]
        else:
            stat_out[h : h + 1, :] = top
            stat_out[heads + h : heads + h + 1, :] = total
            acc_out[cols, :] = acc


def project_kernel(bit, own, got, weight, *rest):
    came, out = rest[:-1], rest[-1]
    width, columns = own.shape[1], out.shape[1]
    mine, other = halves(width)
    start = pl.multiple_of((lax.axis_index("head") ^ bit) * columns, HD)
    share = jnp.dot(
        own[...],
        weight[pl.ds(mine, width), pl.ds(start, columns)],
        preferred_element_type=jnp.float32,
    ) + jnp.dot(
        got[...],
        weight[pl.ds(other, width), pl.ds(start, columns)],
        preferred_element_type=jnp.float32,
    )
    for block in came:
        share = share + block[...].astype(jnp.float32)
    out[...] = share.astype(out.dtype)


SMEM = pl.BlockSpec(memory_space=pltpu.SMEM)
VMEM = pl.BlockSpec(memory_space=pltpu.VMEM)
ANY = pl.BlockSpec(memory_space=pl.ANY)


def call(kernel, in_specs, outs, scratch=(), out_spec=VMEM, flops=0, moved=0, exps=0):
    shapes = [jax.ShapeDtypeStruct(shape, dtype) for shape, dtype in outs]
    return pl.pallas_call(
        kernel,
        out_shape=shapes,
        in_specs=in_specs,
        out_specs=[out_spec] * len(shapes),
        scratch_shapes=list(scratch),
        compiler_params=pltpu.CompilerParams(vmem_limit_bytes=VMEM_LIMIT),
        cost_estimate=pl.CostEstimate(flops=1, bytes_accessed=1, transcendentals=0),
    )


def dma(count):
    return pltpu.SemaphoreType.DMA((count,))


def later(block, *after):
    return pl.pallas_call(
        after_kernel,
        out_shape=jax.ShapeDtypeStruct(block.shape, block.dtype),
        in_specs=[ANY] * (1 + len(after)),
        out_specs=ANY,
        input_output_aliases={0: 0},
    )(block, *after)


def paired_device(
    queries,
    key_rows,
    value_rows,
    ref_keys,
    ref_values,
    key_lists,
    list_counts,
    owner_index,
    out_weight,
    residual,
    gate_scale,
):
    bf16, f32 = jnp.bfloat16, jnp.float32
    rows, columns = queries.shape
    width = columns // 2
    heads = width // HD
    style = ref_keys.shape[1]
    frames = lax.axis_size("frame")

    even = [(i, i ^ CORE) for i in range(0, frames, 2)]
    odd = [(i ^ CORE, i) for i in range(0, frames, 2)]
    with jax.named_scope("core_style"):
        from_even = lax.ppermute(ref_values, "frame", even)
        from_odd = lax.ppermute(ref_keys, "frame", odd)

    kv = ((rows, 2 * width), bf16)
    kv_keep, kv_send = call(
        split_kernel, [ANY] * 2, [kv, kv], scratch=[dma(4)], moved=8 * rows * columns
    )(key_rows, value_rows)
    kv_x = swap(kv_send, "frame", ROW, "x_kv")
    kv_y = swap(kv_keep, "frame", COLUMN, "y_kv")
    kv_xy = swap(kv_x, "frame", COLUMN, "xy_kv")

    second = style // 2
    first = style - second
    parts = [((first, width), bf16), ((second, width), bf16)]
    send_a, send_b, keep = call(
        pick_kernel,
        [SMEM] + [ANY] * 4,
        parts + [((style, width), bf16)],
        scratch=[dma(3)],
        moved=8 * style * width,
    )(owner_index, ref_keys, ref_values, from_even, from_odd)
    send_b = later(send_b, kv_x)

    def choose(part, bit, begin, here, came, *after):
        return call(
            functools.partial(choose_kernel, bit, begin),
            [SMEM] + [ANY] * (2 + len(after)),
            [part],
            scratch=[dma(1)],
            moved=4 * part[0][0] * width,
        )(owner_index, here, came, *after)[0]

    x_came = [swap(sent, "frame", ROW, f"x_style_{j}") for j, sent in enumerate((send_a, send_b))]
    q_keep, q_send = call(
        query_kernel,
        [SMEM, SMEM, ANY, ANY],
        [((rows, width), bf16), ((rows + 16, width), bf16)],
        scratch=[dma(2)],
        moved=4 * rows * columns,
    )(key_lists, list_counts, queries, x_came[0])
    q_got = swap(q_send, "frame", ROW, "x_q")

    near = [kv_keep, kv_x, kv_y, kv_xy]
    near = near + [swap(block, "frame", CORE, f"c_kv_{n}") for n, block in enumerate(near)]
    padded = pltpu.VMEM((PAD, width), bf16)
    state = [((width, PAD), f32), ((8, PAD), f32)]

    def frames_of(remote, q):
        return call(
            functools.partial(frames_kernel, remote),
            [SMEM, SMEM] + [VMEM] * 9,
            state,
            scratch=[padded],
            flops=4 * PAD * width * 8 * rows,
            exps=PAD * heads * 8 * rows,
            moved=16 * rows * width * 2,
        )(key_lists, list_counts, q, *near)

    chosen = [
        choose(parts[j], ROW, j * first, keep, x_came[j], *after)
        for j, after in enumerate(((kv_x, kv_y), (kv_xy,)))
    ]
    y_came = [swap(block, "frame", COLUMN, f"y_style_{j}") for j, block in enumerate(chosen)]

    def finish(j, *after):
        held = choose(parts[j], COLUMN, 0, chosen[j], y_came[j], *after)
        return held, swap(held, "frame", CORE, f"c_style_{j}")

    def style_of(last, j, q, blocks, held_state):
        part = parts[j]
        count = part[0][0]
        return call(
            functools.partial(style_kernel, last, rows),
            [VMEM] * 5,
            [((rows, width), bf16)] if last else state,
            scratch=[pltpu.VMEM(*part), pltpu.VMEM(*part), padded],
            flops=4 * PAD * width * count,
            exps=PAD * heads * count,
            moved=8 * count * width,
        )(q, *blocks, *held_state)

    own_state = frames_of(False, q_keep)
    blocks = finish(0, chosen[1], q_got, own_state[1])
    their_state = frames_of(True, q_got)
    own_state = style_of(False, 0, q_keep, blocks, own_state)
    their_state = style_of(False, 0, q_got, blocks, their_state)
    blocks = finish(1, own_state[1], their_state[1])
    (theirs,) = style_of(True, 1, q_got, blocks, their_state)
    got = swap(theirs, "frame", ROW, "x_back")
    (own,) = style_of(True, 1, q_keep, blocks, own_state)

    def project(bit, dtype, *came):
        return call(
            functools.partial(project_kernel, bit),
            [VMEM] * (3 + len(came)),
            [((rows, columns), dtype)],
            flops=2 * rows * columns * columns,
            moved=2 * columns * columns,
        )(own, got, out_weight, *came)[0]

    relay = swap(project(3, bf16), "head", 1, "z_relay")
    near_share = swap(project(1, bf16), "head", 1, "z_near")
    far_share = swap(project(2, bf16, relay), "head", 2, "z_far")
    projected = project(0, f32) + near_share.astype(f32) + far_share.astype(f32)
    return (residual.astype(f32) + gate_scale[None, :] * projected).astype(bf16)


def solution(mesh):
    placed = (
        P("frame", "head"),
        P("frame", "head"),
        P("frame", "head"),
        P("frame", None, "head"),
        P("frame", None, "head"),
        P("frame", None),
        P("frame"),
        P(),
        P("head", None),
        P("frame", "head"),
        P("head"),
    )

    def per_device(*args):
        rows, columns = args[0].shape
        style = args[3].shape[1]
        paired = (
            mesh.shape["frame"] == 8
            and mesh.shape["head"] == 4
            and columns % (2 * HD) == 0
            and columns // HD <= 8
            and rows % 16 == 0
            and rows <= PAD
            and style % 256 == 0
        )
        return (paired_device if paired else general_device)(*args)

    return jax.shard_map(
        per_device, mesh=mesh, in_specs=placed, out_specs=P("frame", "head"), check_vma=False
    )
```

```python
import functools
import math

import jax
import jax.numpy as jnp
from jax import lax
from jax.experimental import pallas as pl
from jax.experimental.pallas import tpu as pltpu
from jax.sharding import PartitionSpec as P

HD = 128
REACH = 4
LOG2E = 1.4426950408889634
VMEM_LIMIT = 24 * 1024 * 1024


def broadcast(block, axis, source):
    block = jnp.where(lax.axis_index(axis) == source, block, jnp.zeros_like(block))
    return lax.psum(block, axis)


def from_behind(block, axis, distance):
    devices = range(lax.axis_size(axis))
    route = [(i - distance, i) for i in devices if i - distance in devices]
    return lax.ppermute(block, axis, route)


def absorb(carried, query_heads, key_block, value_block, allowed):
    running_max, running_sum, weighted = carried
    head_count = query_heads.shape[1]
    key_heads = key_block.reshape(key_block.shape[0], head_count, HD)
    value_heads = value_block.reshape(value_block.shape[0], head_count, HD)
    scores = jnp.einsum(
        "qhd,khd->hqk", query_heads, key_heads, preferred_element_type=jnp.float32
    ) * (1.0 / math.sqrt(HD))
    if allowed is not None:
        scores = jnp.where(allowed[None, None, :], scores, -jnp.inf)
    new_max = jnp.maximum(running_max, jnp.max(scores, axis=-1))
    factor = jnp.exp(running_max - new_max)
    weights = jnp.exp(scores - new_max[:, :, None])
    running_sum = running_sum * factor + jnp.sum(weights, axis=-1)
    weighted = weighted * factor.T[:, :, None] + jnp.einsum(
        "hqk,khd->qhd",
        weights.astype(jnp.bfloat16),
        value_heads,
        preferred_element_type=jnp.float32,
    )
    return (new_max, running_sum, weighted)


def frame_block(carried, query_heads, key_block, value_block, begin_row, listed, live_slots):
    frame_of = (begin_row + jnp.arange(key_block.shape[0], dtype=jnp.int32)) // query_heads.shape[0]
    allowed = jnp.any((frame_of[:, None] == listed[None, :]) & live_slots[None, :], axis=1)
    return lax.cond(
        jnp.any(allowed),
        lambda current: absorb(current, query_heads, key_block, value_block, allowed),
        lambda current: current,
        carried,
    )


def general_device(
    queries,
    key_rows,
    value_rows,
    ref_keys,
    ref_values,
    key_lists,
    list_counts,
    owner_index,
    out_weight,
    residual,
    gate_scale,
):
    frame_len = queries.shape[0]
    columns_here = queries.shape[1]
    head_count = columns_here // HD
    query_heads = queries.reshape(frame_len, head_count, HD)
    listed = key_lists[0]
    live_slots = jnp.arange(listed.shape[0], dtype=jnp.int32) < list_counts[0]
    position = lax.axis_index("frame")
    carried = (
        jnp.full((head_count, frame_len), -jnp.inf, jnp.float32),
        jnp.zeros((head_count, frame_len), jnp.float32),
        jnp.zeros((frame_len, head_count, HD), jnp.float32),
    )
    style_keys, style_values = (
        broadcast(ref_keys, "frame", owner_index[0]),
        broadcast(ref_values, "frame", owner_index[0]),
    )
    carried = absorb(carried, query_heads, style_keys[0], style_values[0], None)
    carried = absorb(carried, query_heads, key_rows, value_rows, None)
    for offset in list(range(1, REACH + 1)) + list(range(-REACH, 0)):
        moved_keys, moved_values = from_behind((key_rows, value_rows), "frame", offset)
        carried = frame_block(
            carried,
            query_heads,
            moved_keys,
            moved_values,
            (position - offset) * frame_len,
            listed,
            live_slots,
        )
    running_max, running_sum, weighted = carried
    attended = (
        (weighted / running_sum.T[:, :, None]).astype(jnp.bfloat16).reshape(frame_len, columns_here)
    )
    shares = lax.psum_scatter(
        lax.dot_general(
            out_weight, attended, (((0,), (1,)), ((), ())), preferred_element_type=jnp.float32
        ).astype(jnp.bfloat16),
        "head",
        scatter_dimension=0,
        tiled=True,
    ).astype(jnp.float32)
    return (residual.astype(jnp.float32) + gate_scale[None, :] * shares.T).astype(jnp.bfloat16)


CORE, ROW, COLUMN = 1, 2, 4
SLOTS = (0, 2, 4, 6, 1, 3, 5, 7)


def swap(block, axis, bit, name):
    with jax.named_scope(name):
        return lax.ppermute(block, axis, [(i, i ^ bit) for i in range(lax.axis_size(axis))])


def halves(width):
    x = (lax.axis_index("frame") // ROW) % 2
    mine = pl.multiple_of(x * width, HD)
    other = pl.multiple_of((1 - x) * width, HD)
    return mine, other


def visible(frame, lists, counts):
    seen = frame == lax.axis_index("frame")
    for j in range(lists.shape[1]):
        seen = seen | ((lists[0, j] == frame) & (j < counts[0]))
    return seen


def split_kernel(k, v, keep, send, sems):
    rows, width = keep.shape[0], keep.shape[1] // 2
    mine, other = halves(width)
    left, right = pl.ds(0, width), pl.ds(width, width)
    move(
        sems,
        (k.at[:, pl.ds(other, width)], send.at[:, left]),
        (v.at[:, pl.ds(other, width)], send.at[:, right]),
        (k.at[:, pl.ds(mine, width)], keep.at[:, left]),
        (v.at[:, pl.ds(mine, width)], keep.at[:, right]),
    )


def query_kernel(lists, counts, q, after, keep, send, sems):
    rows, width = keep.shape
    mine, other = halves(width)
    lane = lax.broadcasted_iota(jnp.int32, (16, width), 1)
    flags = jnp.zeros((16, width), jnp.float32)
    for g in range(lax.axis_size("frame")):
        flag = jnp.where(visible(g, lists, counts), 1.0, 0.0)
        flags = jnp.where(lane == g, flag, flags)
    send[rows:, :] = flags.astype(jnp.bfloat16)
    move(
        sems,
        (q.at[:, pl.ds(mine, width)], keep),
        (q.at[:, pl.ds(other, width)], send.at[pl.ds(0, rows)]),
    )


def from_owner(owner, k, v, from_even, from_odd, take):
    core = lax.axis_index("frame") % 2
    owner_core = owner[0] % 2
    for at, here, there in ((0, k, from_odd), (1, v, from_even)):
        pl.when((core == at) & (owner_core == at))(functools.partial(take, here))
        pl.when((core == at) & (owner_core != at))(functools.partial(take, there))


def move(sems, *pairs):
    copies = [pltpu.make_async_copy(src, dst, sems.at[i]) for i, (src, dst) in enumerate(pairs)]
    for copy in copies:
        copy.start()
    for copy in copies:
        copy.wait()


def pick_kernel(owner, k, v, from_even, from_odd, send_a, send_b, keep, sems):
    first, width = send_a.shape
    second = send_b.shape[0]
    mine, other = halves(width)

    def take(src):
        move(
            sems,
            (src.at[0, pl.ds(0, first), pl.ds(other, width)], send_a),
            (src.at[0, pl.ds(first, second), pl.ds(other, width)], send_b),
            (src.at[0, :, pl.ds(mine, width)], keep),
        )

    from_owner(owner, k, v, from_even, from_odd, take)


def hold_kernel(block, *rest):
    out, sems = rest[-2:]
    move(sems, (block, out))


def choose_kernel(bit, begin, owner, here, came, *rest):
    out, sems = rest[-2:]
    own = (owner[0] // bit) % 2 == (lax.axis_index("frame") // bit) % 2

    @pl.when(own)
    def _():
        move(sems, (here.at[pl.ds(begin, out.shape[0])], out))

    @pl.when(jnp.logical_not(own))
    def _():
        move(sems, (came, out))


NT = (((1,), (1,)), ((), ()))


def absorb_chunk(query, keys, values, biases, state):
    scale = LOG2E / math.sqrt(HD)
    scores = [lax.dot_general(query, k, NT, preferred_element_type=jnp.float32) for k in keys]
    top = None
    for s, b in zip(scores, biases):
        t = jnp.max(s, axis=1, keepdims=True) * scale + b
        top = t if top is None else jnp.maximum(top, t)
    if state is not None:
        old_top, old_sum, old_acc = state
        top = jnp.maximum(old_top, top)
    total, acc = None, None
    for s, b, v in zip(scores, biases, values):
        p = jnp.exp2(s * scale - (top - b))
        part = jnp.sum(p, axis=1, keepdims=True)
        total = part if total is None else total + part
        o = jnp.dot(p.astype(jnp.bfloat16), v, preferred_element_type=jnp.float32)
        acc = o if acc is None else acc + o
    if state is not None:
        factor = jnp.exp2(old_top - top)
        total = total + old_sum * factor
        acc = acc + old_acc * factor
    return top, total, acc


def store_state(acc_out, stat_out, h, state):
    heads = acc_out.shape[1] // HD
    stat_out[:, h : h + 1] = state[0]
    stat_out[:, heads + h : heads + h + 1] = state[1]
    acc_out[:, h * HD : (h + 1) * HD] = state[2]


def frames_kernel(remote, lists, counts, q, *rest):
    kv = rest[: len(SLOTS)]
    acc_out, stat_out = rest[len(SLOTS) :]
    rows, width = kv[0].shape[0], kv[0].shape[1] // 2
    here = lax.axis_index("frame")
    if remote:
        flags = q[rows : rows + 16, :].astype(jnp.float32)
        lane = lax.broadcasted_iota(jnp.int32, (16, width), 1)
    biases = []
    for bit in SLOTS:
        frame = here ^ bit
        if remote:
            seen = jnp.max(jnp.where(lane == frame, flags, 0.0), keepdims=True)
            biases.append(jnp.where(seen > 0.5, 0.0, -jnp.inf))
        else:
            biases.append(jnp.where(visible(frame, lists, counts), 0.0, -jnp.inf))
    group = 4
    for h in range(width // HD):
        keys = slice(h * HD, (h + 1) * HD)
        values = slice(width + h * HD, width + (h + 1) * HD)
        state = None
        for s in range(0, len(SLOTS), group):
            blocks = kv[s : s + group]
            state = absorb_chunk(
                q[:rows, keys],
                [block[:, keys] for block in blocks],
                [block[:, values] for block in blocks],
                biases[s : s + group],
                state,
            )
        store_state(acc_out, stat_out, h, state)


def style_kernel(last, q, held, swapped, acc_in, stat_in, *outs):
    rows, width = acc_in.shape
    heads = width // HD
    core = lax.axis_index("frame") % 2

    def run(keys, values):
        for h in range(heads):
            cols = slice(h * HD, (h + 1) * HD)
            state = (stat_in[:, h : h + 1], stat_in[:, heads + h : heads + h + 1], acc_in[:, cols])
            state = absorb_chunk(
                q[:rows, cols], [keys[:, cols]], [values[:, cols]], [0.0], state
            )
            if last:
                outs[0][:, cols] = (state[2] / state[1]).astype(jnp.bfloat16)
            else:
                store_state(*outs, h, state)

    pl.when(core == 0)(functools.partial(run, held, swapped))
    pl.when(core == 1)(functools.partial(run, swapped, held))


def project_kernel(bit, own, got, weight, *rest):
    came, out = rest[:-1], rest[-1]
    width, columns = own.shape[1], out.shape[1]
    mine, other = halves(width)
    start = pl.multiple_of((lax.axis_index("head") ^ bit) * columns, HD)
    share = jnp.dot(
        own[...],
        weight[pl.ds(mine, width), pl.ds(start, columns)],
        preferred_element_type=jnp.float32,
    ) + jnp.dot(
        got[...],
        weight[pl.ds(other, width), pl.ds(start, columns)],
        preferred_element_type=jnp.float32,
    )
    for block in came:
        share = share + block[...].astype(jnp.float32)
    out[...] = share.astype(out.dtype)


SMEM = pl.BlockSpec(memory_space=pltpu.SMEM)
VMEM = pl.BlockSpec(memory_space=pltpu.VMEM)
ANY = pl.BlockSpec(memory_space=pl.ANY)


def call(kernel, in_specs, outs, scratch=(), out_spec=VMEM):
    shapes = [jax.ShapeDtypeStruct(shape, dtype) for shape, dtype in outs]
    return pl.pallas_call(
        kernel,
        out_shape=shapes,
        in_specs=in_specs,
        out_specs=[out_spec] * len(shapes),
        scratch_shapes=list(scratch),
        compiler_params=pltpu.CompilerParams(vmem_limit_bytes=VMEM_LIMIT),
        cost_estimate=pl.CostEstimate(flops=1, bytes_accessed=1, transcendentals=0),
    )


def dma(count):
    return pltpu.SemaphoreType.DMA((count,))


def later(block, *after):
    return call(
        hold_kernel, [ANY] * (1 + len(after)), [(block.shape, block.dtype)], scratch=[dma(1)]
    )(block, *after)[0]


def paired_device(
    queries,
    key_rows,
    value_rows,
    ref_keys,
    ref_values,
    key_lists,
    list_counts,
    owner_index,
    out_weight,
    residual,
    gate_scale,
):
    bf16, f32 = jnp.bfloat16, jnp.float32
    rows, columns = queries.shape
    width = columns // 2
    heads = width // HD
    style = ref_keys.shape[1]
    frames = lax.axis_size("frame")

    even = [(i, i ^ CORE) for i in range(0, frames, 2)]
    odd = [(i ^ CORE, i) for i in range(0, frames, 2)]
    with jax.named_scope("core_style"):
        from_even = lax.ppermute(ref_values, "frame", even)
        from_odd = lax.ppermute(ref_keys, "frame", odd)

    kv = ((rows, 2 * width), bf16)
    kv_keep, kv_send = call(
        split_kernel, [ANY] * 2, [kv, kv], scratch=[dma(4)]
    )(key_rows, value_rows)
    kv_x = swap(kv_send, "frame", ROW, "x_kv")
    kv_y = swap(kv_keep, "frame", COLUMN, "y_kv")
    kv_xy = swap(kv_x, "frame", COLUMN, "xy_kv")

    second = style // 2
    first = style - second
    parts = [((first, width), bf16), ((second, width), bf16)]
    send_a, send_b, keep = call(
        pick_kernel,
        [SMEM] + [ANY] * 4,
        parts + [((style, width), bf16)],
        scratch=[dma(3)],
    )(owner_index, ref_keys, ref_values, from_even, from_odd)
    send_b = later(send_b, kv_x)

    def choose(part, bit, begin, here, came, *after):
        return call(
            functools.partial(choose_kernel, bit, begin),
            [SMEM] + [ANY] * (2 + len(after)),
            [part],
            scratch=[dma(1)],
        )(owner_index, here, came, *after)[0]

    x_came = [swap(sent, "frame", ROW, f"x_style_{j}") for j, sent in enumerate((send_a, send_b))]
    q_keep, q_send = call(
        query_kernel,
        [SMEM, SMEM, ANY, ANY],
        [((rows, width), bf16), ((rows + 16, width), bf16)],
        scratch=[dma(2)],
    )(key_lists, list_counts, queries, kv_x)
    q_got = swap(q_send, "frame", ROW, "x_q")

    near = [kv_keep, kv_x, kv_y, kv_xy]
    near = near + [swap(block, "frame", CORE, f"c_kv_{n}") for n, block in enumerate(near)]
    state = [((rows, width), f32), ((rows, HD), f32)]

    def frames_of(remote, q):
        return call(
            functools.partial(frames_kernel, remote),
            [SMEM, SMEM] + [VMEM] * 9,
            state,
        )(key_lists, list_counts, q, *near)

    chosen = [
        choose(parts[j], ROW, j * first, keep, x_came[j], *after)
        for j, after in enumerate(((kv_x, kv_y), (kv_xy,)))
    ]
    y_came = [swap(block, "frame", COLUMN, f"y_style_{j}") for j, block in enumerate(chosen)]

    def finish(j, *after):
        held = choose(parts[j], COLUMN, 0, chosen[j], y_came[j], *after)
        return held, swap(held, "frame", CORE, f"c_style_{j}")

    def style_of(last, j, q, blocks, held_state):
        return call(
            functools.partial(style_kernel, last),
            [VMEM] * 5,
            [((rows, width), bf16)] if last else state,
        )(q, *blocks, *held_state)

    own_state = frames_of(False, q_keep)
    their_state = frames_of(True, q_got)
    seen = own_state[1], their_state[1]
    blocks = finish(0, chosen[1], q_got)
    own_state = style_of(False, 0, q_keep, blocks, own_state)
    their_state = style_of(False, 0, q_got, blocks, their_state)
    blocks = finish(1, *seen)
    (theirs,) = style_of(True, 1, q_got, blocks, their_state)
    got = swap(theirs, "frame", ROW, "x_back")
    (own,) = style_of(True, 1, q_keep, blocks, own_state)

    def project(bit, dtype, *came):
        return call(
            functools.partial(project_kernel, bit),
            [VMEM] * (3 + len(came)),
            [((rows, columns), dtype)],
        )(own, got, out_weight, *came)[0]

    relay = swap(project(3, bf16), "head", 1, "z_relay")
    near_share = swap(project(1, bf16), "head", 1, "z_near")
    far_share = swap(project(2, bf16, relay), "head", 2, "z_far")
    projected = project(0, f32) + near_share.astype(f32) + far_share.astype(f32)
    return (residual.astype(f32) + gate_scale[None, :] * projected).astype(bf16)


def solution(mesh):
    placed = (
        P("frame", "head"),
        P("frame", "head"),
        P("frame", "head"),
        P("frame", None, "head"),
        P("frame", None, "head"),
        P("frame", None),
        P("frame"),
        P(),
        P("head", None),
        P("frame", "head"),
        P("head"),
    )

    def per_device(*args):
        rows, columns = args[0].shape
        style = args[3].shape[1]
        paired = (
            mesh.shape["frame"] == 8
            and mesh.shape["head"] == 4
            and columns % (2 * HD) == 0
            and columns // HD <= HD
            and rows % 16 == 0
            and style % 256 == 0
        )
        return (paired_device if paired else general_device)(*args)

    return jax.shard_map(
        per_device, mesh=mesh, in_specs=placed, out_specs=P("frame", "head"), check_vma=False
    )
```

```python
import functools
import math

import jax
import jax.numpy as jnp
from jax import lax
from jax.experimental import pallas as pl
from jax.experimental.pallas import tpu as pltpu
from jax.sharding import PartitionSpec as P

HD = 128
REACH = 4
LOG2E = 1.4426950408889634
VMEM_LIMIT = 24 * 1024 * 1024


def broadcast(block, axis, source):
    block = jnp.where(lax.axis_index(axis) == source, block, jnp.zeros_like(block))
    return lax.psum(block, axis)


def from_behind(block, axis, distance):
    devices = range(lax.axis_size(axis))
    route = [(i - distance, i) for i in devices if i - distance in devices]
    return lax.ppermute(block, axis, route)


def absorb(carried, query_heads, key_block, value_block, allowed):
    running_max, running_sum, weighted = carried
    head_count = query_heads.shape[1]
    key_heads = key_block.reshape(key_block.shape[0], head_count, HD)
    value_heads = value_block.reshape(value_block.shape[0], head_count, HD)
    scores = jnp.einsum(
        "qhd,khd->hqk", query_heads, key_heads, preferred_element_type=jnp.float32
    ) * (1.0 / math.sqrt(HD))
    if allowed is not None:
        scores = jnp.where(allowed[None, None, :], scores, -jnp.inf)
    new_max = jnp.maximum(running_max, jnp.max(scores, axis=-1))
    factor = jnp.exp(running_max - new_max)
    weights = jnp.exp(scores - new_max[:, :, None])
    running_sum = running_sum * factor + jnp.sum(weights, axis=-1)
    weighted = weighted * factor.T[:, :, None] + jnp.einsum(
        "hqk,khd->qhd",
        weights.astype(jnp.bfloat16),
        value_heads,
        preferred_element_type=jnp.float32,
    )
    return (new_max, running_sum, weighted)


def frame_block(carried, query_heads, key_block, value_block, begin_row, listed, live_slots):
    frame_of = (begin_row + jnp.arange(key_block.shape[0], dtype=jnp.int32)) // query_heads.shape[0]
    allowed = jnp.any((frame_of[:, None] == listed[None, :]) & live_slots[None, :], axis=1)
    return lax.cond(
        jnp.any(allowed),
        lambda current: absorb(current, query_heads, key_block, value_block, allowed),
        lambda current: current,
        carried,
    )


def general_device(
    queries,
    key_rows,
    value_rows,
    ref_keys,
    ref_values,
    key_lists,
    list_counts,
    owner_index,
    out_weight,
    residual,
    gate_scale,
):
    frame_len = queries.shape[0]
    columns_here = queries.shape[1]
    head_count = columns_here // HD
    query_heads = queries.reshape(frame_len, head_count, HD)
    listed = key_lists[0]
    live_slots = jnp.arange(listed.shape[0], dtype=jnp.int32) < list_counts[0]
    position = lax.axis_index("frame")
    carried = (
        jnp.full((head_count, frame_len), -jnp.inf, jnp.float32),
        jnp.zeros((head_count, frame_len), jnp.float32),
        jnp.zeros((frame_len, head_count, HD), jnp.float32),
    )
    style_keys, style_values = (
        broadcast(ref_keys, "frame", owner_index[0]),
        broadcast(ref_values, "frame", owner_index[0]),
    )
    carried = absorb(carried, query_heads, style_keys[0], style_values[0], None)
    carried = absorb(carried, query_heads, key_rows, value_rows, None)
    for offset in list(range(1, REACH + 1)) + list(range(-REACH, 0)):
        moved_keys, moved_values = from_behind((key_rows, value_rows), "frame", offset)
        carried = frame_block(
            carried,
            query_heads,
            moved_keys,
            moved_values,
            (position - offset) * frame_len,
            listed,
            live_slots,
        )
    running_max, running_sum, weighted = carried
    attended = (
        (weighted / running_sum.T[:, :, None]).astype(jnp.bfloat16).reshape(frame_len, columns_here)
    )
    shares = lax.psum_scatter(
        lax.dot_general(
            out_weight, attended, (((0,), (1,)), ((), ())), preferred_element_type=jnp.float32
        ).astype(jnp.bfloat16),
        "head",
        scatter_dimension=0,
        tiled=True,
    ).astype(jnp.float32)
    return (residual.astype(jnp.float32) + gate_scale[None, :] * shares.T).astype(jnp.bfloat16)


CORE, ROW, COLUMN = 1, 2, 4
SLOTS = (0, 2, 4, 6, 1, 3, 5, 7)


def swap(block, axis, bit, name):
    with jax.named_scope(name):
        return lax.ppermute(block, axis, [(i, i ^ bit) for i in range(lax.axis_size(axis))])


def halves(width):
    x = (lax.axis_index("frame") // ROW) % 2
    mine = pl.multiple_of(x * width, HD)
    other = pl.multiple_of((1 - x) * width, HD)
    return mine, other


def visible(frame, lists, counts):
    seen = frame == lax.axis_index("frame")
    for j in range(lists.shape[1]):
        seen = seen | ((lists[0, j] == frame) & (j < counts[0]))
    return seen


def split_kernel(k, v, keep, send, sems):
    rows, width = keep.shape[0], keep.shape[1] // 2
    mine, other = halves(width)
    left, right = pl.ds(0, width), pl.ds(width, width)
    move(
        sems,
        (k.at[:, pl.ds(other, width)], send.at[:, left]),
        (v.at[:, pl.ds(other, width)], send.at[:, right]),
        (k.at[:, pl.ds(mine, width)], keep.at[:, left]),
        (v.at[:, pl.ds(mine, width)], keep.at[:, right]),
    )


def query_kernel(lists, counts, q, after, keep, send, sems):
    rows, width = keep.shape
    mine, other = halves(width)
    lane = lax.broadcasted_iota(jnp.int32, (16, width), 1)
    flags = jnp.zeros((16, width), jnp.float32)
    for g in range(lax.axis_size("frame")):
        flag = jnp.where(visible(g, lists, counts), 1.0, 0.0)
        flags = jnp.where(lane == g, flag, flags)
    send[rows:, :] = flags.astype(jnp.bfloat16)
    move(
        sems,
        (q.at[:, pl.ds(mine, width)], keep),
        (q.at[:, pl.ds(other, width)], send.at[pl.ds(0, rows)]),
    )


def from_owner(owner, k, v, from_even, from_odd, take):
    core = lax.axis_index("frame") % 2
    owner_core = owner[0] % 2
    for at, here, there in ((0, k, from_odd), (1, v, from_even)):
        pl.when((core == at) & (owner_core == at))(functools.partial(take, here))
        pl.when((core == at) & (owner_core != at))(functools.partial(take, there))


def move(sems, *pairs):
    copies = [pltpu.make_async_copy(src, dst, sems.at[i]) for i, (src, dst) in enumerate(pairs)]
    for copy in copies:
        copy.start()
    for copy in copies:
        copy.wait()


def pick_kernel(owner, k, v, from_even, from_odd, after, send_a, send_b, keep, sems):
    first, width = send_a.shape
    second = send_b.shape[0]
    mine, other = halves(width)

    def take(src):
        move(
            sems,
            (src.at[0, pl.ds(0, first), pl.ds(other, width)], send_a),
            (src.at[0, pl.ds(first, second), pl.ds(other, width)], send_b),
            (src.at[0, :, pl.ds(mine, width)], keep),
        )

    from_owner(owner, k, v, from_even, from_odd, take)


def hold_kernel(block, *rest):
    out, sems = rest[-2:]
    move(sems, (block, out))


def choose_kernel(bit, begin, owner, here, came, *rest):
    out, sems = rest[-2:]
    own = (owner[0] // bit) % 2 == (lax.axis_index("frame") // bit) % 2

    @pl.when(own)
    def _():
        move(sems, (here.at[pl.ds(begin, out.shape[0])], out))

    @pl.when(jnp.logical_not(own))
    def _():
        move(sems, (came, out))


NT = (((1,), (1,)), ((), ()))


def absorb_chunk(query, keys, values, biases, state):
    scale = LOG2E / math.sqrt(HD)
    scores = [lax.dot_general(query, k, NT, preferred_element_type=jnp.float32) for k in keys]
    top = None
    for s, b in zip(scores, biases):
        t = jnp.max(s, axis=1, keepdims=True) * scale + b
        top = t if top is None else jnp.maximum(top, t)
    if state is not None:
        old_top, old_sum, old_acc = state
        top = jnp.maximum(old_top, top)
    total, acc = None, None
    for s, b, v in zip(scores, biases, values):
        p = jnp.exp2(s * scale - (top - b))
        part = jnp.sum(p, axis=1, keepdims=True)
        total = part if total is None else total + part
        o = jnp.dot(p.astype(jnp.bfloat16), v, preferred_element_type=jnp.float32)
        acc = o if acc is None else acc + o
    if state is not None:
        factor = jnp.exp2(old_top - top)
        total = total + old_sum * factor
        acc = acc + old_acc * factor
    return top, total, acc


def store_state(acc_out, stat_out, h, state):
    heads = acc_out.shape[1] // HD
    stat_out[:, h : h + 1] = state[0]
    stat_out[:, heads + h : heads + h + 1] = state[1]
    acc_out[:, h * HD : (h + 1) * HD] = state[2]


def frames_kernel(remote, lists, counts, q, *rest):
    kv = rest[: len(SLOTS)]
    acc_out, stat_out = rest[len(SLOTS) :]
    rows, width = kv[0].shape[0], kv[0].shape[1] // 2
    here = lax.axis_index("frame")
    if remote:
        flags = q[rows : rows + 16, :].astype(jnp.float32)
        lane = lax.broadcasted_iota(jnp.int32, (16, width), 1)
    biases = []
    for bit in SLOTS:
        frame = here ^ bit
        if remote:
            seen = jnp.max(jnp.where(lane == frame, flags, 0.0), keepdims=True)
            biases.append(jnp.where(seen > 0.5, 0.0, -jnp.inf))
        else:
            biases.append(jnp.where(visible(frame, lists, counts), 0.0, -jnp.inf))
    group = 4
    for h in range(width // HD):
        keys = slice(h * HD, (h + 1) * HD)
        values = slice(width + h * HD, width + (h + 1) * HD)
        state = None
        for s in range(0, len(SLOTS), group):
            blocks = kv[s : s + group]
            state = absorb_chunk(
                q[:rows, keys],
                [block[:, keys] for block in blocks],
                [block[:, values] for block in blocks],
                biases[s : s + group],
                state,
            )
        store_state(acc_out, stat_out, h, state)


def style_kernel(last, q, held, swapped, acc_in, stat_in, *outs):
    rows, width = acc_in.shape
    heads = width // HD
    core = lax.axis_index("frame") % 2

    def run(keys, values):
        for h in range(heads):
            cols = slice(h * HD, (h + 1) * HD)
            state = (stat_in[:, h : h + 1], stat_in[:, heads + h : heads + h + 1], acc_in[:, cols])
            state = absorb_chunk(
                q[:rows, cols], [keys[:, cols]], [values[:, cols]], [0.0], state
            )
            if last:
                outs[0][:, cols] = (state[2] / state[1]).astype(jnp.bfloat16)
            else:
                store_state(*outs, h, state)

    pl.when(core == 0)(functools.partial(run, held, swapped))
    pl.when(core == 1)(functools.partial(run, swapped, held))


def project_kernel(bit, own, got, weight, *rest):
    came, out = rest[:-1], rest[-1]
    width, columns = own.shape[1], out.shape[1]
    mine, other = halves(width)
    start = pl.multiple_of((lax.axis_index("head") ^ bit) * columns, HD)
    share = jnp.dot(
        own[...],
        weight[pl.ds(mine, width), pl.ds(start, columns)],
        preferred_element_type=jnp.float32,
    ) + jnp.dot(
        got[...],
        weight[pl.ds(other, width), pl.ds(start, columns)],
        preferred_element_type=jnp.float32,
    )
    for block in came:
        share = share + block[...].astype(jnp.float32)
    out[...] = share.astype(out.dtype)


SMEM = pl.BlockSpec(memory_space=pltpu.SMEM)
VMEM = pl.BlockSpec(memory_space=pltpu.VMEM)
ANY = pl.BlockSpec(memory_space=pl.ANY)


def call(kernel, in_specs, outs, scratch=(), out_spec=VMEM, flops=1):
    shapes = [jax.ShapeDtypeStruct(shape, dtype) for shape, dtype in outs]
    return pl.pallas_call(
        kernel,
        out_shape=shapes,
        in_specs=in_specs,
        out_specs=[out_spec] * len(shapes),
        scratch_shapes=list(scratch),
        compiler_params=pltpu.CompilerParams(vmem_limit_bytes=VMEM_LIMIT),
        cost_estimate=pl.CostEstimate(flops=flops, bytes_accessed=1, transcendentals=0),
    )


def dma(count):
    return pltpu.SemaphoreType.DMA((count,))


def later(block, *after, flops=1):
    return call(
        hold_kernel, [ANY] * (1 + len(after)), [(block.shape, block.dtype)], scratch=[dma(1)], flops=flops
    )(block, *after)[0]


def paired_device(
    queries,
    key_rows,
    value_rows,
    ref_keys,
    ref_values,
    key_lists,
    list_counts,
    owner_index,
    out_weight,
    residual,
    gate_scale,
):
    bf16, f32 = jnp.bfloat16, jnp.float32
    rows, columns = queries.shape
    width = columns // 2
    heads = width // HD
    style = ref_keys.shape[1]
    frames = lax.axis_size("frame")

    even = [(i, i ^ CORE) for i in range(0, frames, 2)]
    odd = [(i ^ CORE, i) for i in range(0, frames, 2)]
    with jax.named_scope("core_style"):
        from_even = lax.ppermute(ref_values, "frame", even)
        from_odd = lax.ppermute(ref_keys, "frame", odd)

    right = (lax.axis_index("frame") // ROW) % 2 == 1

    def half_of(block, flag):
        return jnp.where(flag, block[:, width:], block[:, :width])

    kv_send, kv_keep = [
        jnp.concatenate([half_of(key_rows, flag), half_of(value_rows, flag)], axis=1)
        for flag in (jnp.logical_not(right), right)
    ]
    kv_x = swap(kv_send, "frame", ROW, "x_kv")
    kv_y = swap(kv_keep, "frame", COLUMN, "y_kv")
    kv_xy = swap(kv_x, "frame", COLUMN, "xy_kv")

    near = [kv_keep, kv_x, kv_y, kv_xy]
    near = near + [swap(block, "frame", CORE, f"c_kv_{n}") for n, block in enumerate(near)]
    ready = later(kv_x[:16], kv_x, kv_y, flops=4 * 10**10)
    first = style * 16 // 32
    second = style - first
    parts = [((first, width), bf16), ((second, width), bf16)]
    send_a, send_b, keep = call(
        pick_kernel,
        [SMEM] + [ANY] * 5,
        parts + [((style, width), bf16)],
        scratch=[dma(3)],
    )(owner_index, ref_keys, ref_values, from_even, from_odd, ready)
    send_b = later(send_b, near[4])

    def choose(part, bit, begin, here, came, *after):
        return call(
            functools.partial(choose_kernel, bit, begin),
            [SMEM] + [ANY] * (2 + len(after)),
            [part],
            scratch=[dma(1)],
            flops=1,
        )(owner_index, here, came, *after)[0]

    x_came = [swap(sent, "frame", ROW, f"x_style_{j}") for j, sent in enumerate((send_a, send_b))]
    q_keep, q_send = call(
        query_kernel,
        [SMEM, SMEM, ANY, ANY],
        [((rows, width), bf16), ((rows + 16, width), bf16)],
        scratch=[dma(2)],
    )(key_lists, list_counts, queries, kv_y)
    q_got = swap(q_send, "frame", ROW, "x_q")

    state = [((rows, width), f32), ((rows, HD), f32)]

    def frames_of(remote, q):
        return call(
            functools.partial(frames_kernel, remote),
            [SMEM, SMEM] + [VMEM] * 9,
            state,
            flops=3 * 10**9,
        )(key_lists, list_counts, q, *near)

    chosen = [
        choose(parts[j], ROW, j * first, keep, x_came[j], *after)
        for j, after in enumerate(((kv_x,), (kv_xy, *near[4:],)))
    ]
    y_came = [swap(block, "frame", COLUMN, f"y_style_{j}") for j, block in enumerate(chosen)]

    def finish(j, *after):
        held = choose(parts[j], COLUMN, 0, chosen[j], y_came[j], *after)
        return held, swap(held, "frame", CORE, f"c_style_{j}")

    def style_of(last, j, q, blocks, held_state):
        return call(
            functools.partial(style_kernel, last),
            [VMEM] * 5,
            [((rows, width), bf16)] if last else state,
            flops=10**9,
        )(q, *blocks, *held_state)

    own_state = frames_of(False, q_keep)
    their_state = frames_of(True, q_got)
    seen = own_state[1], their_state[1]
    blocks = finish(0, seen[0])
    own_state = style_of(False, 0, q_keep, blocks, own_state)
    their_state = style_of(False, 0, q_got, blocks, their_state)
    blocks = finish(1, *seen)
    (theirs,) = style_of(True, 1, q_got, blocks, their_state)
    got = swap(theirs, "frame", ROW, "x_back")
    (own,) = style_of(True, 1, q_keep, blocks, own_state)

    def project(bit, dtype, *came):
        return call(
            functools.partial(project_kernel, bit),
            [VMEM] * (3 + len(came)),
            [((rows, columns), dtype)],
        )(own, got, out_weight, *came)[0]

    relay = swap(project(3, bf16), "head", 1, "z_relay")
    near_share = swap(project(1, bf16), "head", 1, "z_near")
    far_share = swap(project(2, bf16, relay), "head", 2, "z_far")
    projected = project(0, f32) + near_share.astype(f32) + far_share.astype(f32)
    return (residual.astype(f32) + gate_scale[None, :] * projected).astype(bf16)


def solution(mesh):
    placed = (
        P("frame", "head"),
        P("frame", "head"),
        P("frame", "head"),
        P("frame", None, "head"),
        P("frame", None, "head"),
        P("frame", None),
        P("frame"),
        P(),
        P("head", None),
        P("frame", "head"),
        P("head"),
    )

    def per_device(*args):
        rows, columns = args[0].shape
        style = args[3].shape[1]
        paired = (
            mesh.shape["frame"] == 8
            and mesh.shape["head"] == 4
            and columns % (2 * HD) == 0
            and columns // HD <= HD
            and rows % 16 == 0
            and style % 256 == 0
        )
        return (paired_device if paired else general_device)(*args)

    return jax.shard_map(
        per_device, mesh=mesh, in_specs=placed, out_specs=P("frame", "head"), check_vma=False
    )
```

```python
import functools
import math

import jax
import jax.numpy as jnp
from jax import lax
from jax.experimental import pallas as pl
from jax.experimental.pallas import tpu as pltpu
from jax.sharding import PartitionSpec as P

HD = 128
REACH = 4
LOG2E = 1.4426950408889634
VMEM_LIMIT = 24 * 1024 * 1024


def broadcast(block, axis, source):
    block = jnp.where(lax.axis_index(axis) == source, block, jnp.zeros_like(block))
    return lax.psum(block, axis)


def from_behind(block, axis, distance):
    devices = range(lax.axis_size(axis))
    route = [(i - distance, i) for i in devices if i - distance in devices]
    return lax.ppermute(block, axis, route)


def absorb(carried, query_heads, key_block, value_block, allowed):
    running_max, running_sum, weighted = carried
    head_count = query_heads.shape[1]
    key_heads = key_block.reshape(key_block.shape[0], head_count, HD)
    value_heads = value_block.reshape(value_block.shape[0], head_count, HD)
    scores = jnp.einsum(
        "qhd,khd->hqk", query_heads, key_heads, preferred_element_type=jnp.float32
    ) * (1.0 / math.sqrt(HD))
    if allowed is not None:
        scores = jnp.where(allowed[None, None, :], scores, -jnp.inf)
    new_max = jnp.maximum(running_max, jnp.max(scores, axis=-1))
    factor = jnp.exp(running_max - new_max)
    weights = jnp.exp(scores - new_max[:, :, None])
    running_sum = running_sum * factor + jnp.sum(weights, axis=-1)
    weighted = weighted * factor.T[:, :, None] + jnp.einsum(
        "hqk,khd->qhd",
        weights.astype(jnp.bfloat16),
        value_heads,
        preferred_element_type=jnp.float32,
    )
    return (new_max, running_sum, weighted)


def frame_block(carried, query_heads, key_block, value_block, begin_row, listed, live_slots):
    frame_of = (begin_row + jnp.arange(key_block.shape[0], dtype=jnp.int32)) // query_heads.shape[0]
    allowed = jnp.any((frame_of[:, None] == listed[None, :]) & live_slots[None, :], axis=1)
    return lax.cond(
        jnp.any(allowed),
        lambda current: absorb(current, query_heads, key_block, value_block, allowed),
        lambda current: current,
        carried,
    )


def general_device(
    queries,
    key_rows,
    value_rows,
    ref_keys,
    ref_values,
    key_lists,
    list_counts,
    owner_index,
    out_weight,
    residual,
    gate_scale,
):
    frame_len = queries.shape[0]
    columns_here = queries.shape[1]
    head_count = columns_here // HD
    query_heads = queries.reshape(frame_len, head_count, HD)
    listed = key_lists[0]
    live_slots = jnp.arange(listed.shape[0], dtype=jnp.int32) < list_counts[0]
    position = lax.axis_index("frame")
    carried = (
        jnp.full((head_count, frame_len), -jnp.inf, jnp.float32),
        jnp.zeros((head_count, frame_len), jnp.float32),
        jnp.zeros((frame_len, head_count, HD), jnp.float32),
    )
    style_keys, style_values = (
        broadcast(ref_keys, "frame", owner_index[0]),
        broadcast(ref_values, "frame", owner_index[0]),
    )
    carried = absorb(carried, query_heads, style_keys[0], style_values[0], None)
    carried = absorb(carried, query_heads, key_rows, value_rows, None)
    for offset in list(range(1, REACH + 1)) + list(range(-REACH, 0)):
        moved_keys, moved_values = from_behind((key_rows, value_rows), "frame", offset)
        carried = frame_block(
            carried,
            query_heads,
            moved_keys,
            moved_values,
            (position - offset) * frame_len,
            listed,
            live_slots,
        )
    running_max, running_sum, weighted = carried
    attended = (
        (weighted / running_sum.T[:, :, None]).astype(jnp.bfloat16).reshape(frame_len, columns_here)
    )
    shares = lax.psum_scatter(
        lax.dot_general(
            out_weight, attended, (((0,), (1,)), ((), ())), preferred_element_type=jnp.float32
        ).astype(jnp.bfloat16),
        "head",
        scatter_dimension=0,
        tiled=True,
    ).astype(jnp.float32)
    return (residual.astype(jnp.float32) + gate_scale[None, :] * shares.T).astype(jnp.bfloat16)


CORE, ROW, COLUMN = 1, 2, 4
SLOTS = (0, 2, 4, 6, 1, 3, 5, 7)


def swap(block, axis, bit, name):
    with jax.named_scope(name):
        return lax.ppermute(block, axis, [(i, i ^ bit) for i in range(lax.axis_size(axis))])


def halves(width):
    x = (lax.axis_index("frame") // ROW) % 2
    mine = pl.multiple_of(x * width, HD)
    other = pl.multiple_of((1 - x) * width, HD)
    return mine, other


def visible(frame, lists, counts):
    seen = frame == lax.axis_index("frame")
    for j in range(lists.shape[1]):
        seen = seen | ((lists[0, j] == frame) & (j < counts[0]))
    return seen


def split_kernel(k, v, keep, send, sems):
    rows, width = keep.shape[0], keep.shape[1] // 2
    mine, other = halves(width)
    left, right = pl.ds(0, width), pl.ds(width, width)
    move(
        sems,
        (k.at[:, pl.ds(other, width)], send.at[:, left]),
        (v.at[:, pl.ds(other, width)], send.at[:, right]),
        (k.at[:, pl.ds(mine, width)], keep.at[:, left]),
        (v.at[:, pl.ds(mine, width)], keep.at[:, right]),
    )


def query_kernel(lists, counts, q, after, keep, send, sems):
    rows, width = keep.shape
    mine, other = halves(width)
    lane = lax.broadcasted_iota(jnp.int32, (16, width), 1)
    flags = jnp.zeros((16, width), jnp.float32)
    for g in range(lax.axis_size("frame")):
        flag = jnp.where(visible(g, lists, counts), 1.0, 0.0)
        flags = jnp.where(lane == g, flag, flags)
    send[rows:, :] = flags.astype(jnp.bfloat16)
    move(
        sems,
        (q.at[:, pl.ds(mine, width)], keep),
        (q.at[:, pl.ds(other, width)], send.at[pl.ds(0, rows)]),
    )


def from_owner(owner, k, v, from_even, from_odd, take):
    core = lax.axis_index("frame") % 2
    owner_core = owner[0] % 2
    for at, here, there in ((0, k, from_odd), (1, v, from_even)):
        pl.when((core == at) & (owner_core == at))(functools.partial(take, here))
        pl.when((core == at) & (owner_core != at))(functools.partial(take, there))


def move(sems, *pairs):
    copies = [pltpu.make_async_copy(src, dst, sems.at[i]) for i, (src, dst) in enumerate(pairs)]
    for copy in copies:
        copy.start()
    for copy in copies:
        copy.wait()


def pick_kernel(owner, k, v, from_even, from_odd, after, send_a, send_b, keep, sems):
    first, width = send_a.shape
    second = send_b.shape[0]
    mine, other = halves(width)

    def take(src):
        move(
            sems,
            (src.at[0, pl.ds(0, first), pl.ds(other, width)], send_a),
            (src.at[0, pl.ds(first, second), pl.ds(other, width)], send_b),
            (src.at[0, :, pl.ds(mine, width)], keep),
        )

    from_owner(owner, k, v, from_even, from_odd, take)


def hold_kernel(block, *rest):
    out, sems = rest[-2:]
    move(sems, (block, out))


def choose_kernel(bit, begin, owner, here, came, *rest):
    out, sems = rest[-2:]
    own = (owner[0] // bit) % 2 == (lax.axis_index("frame") // bit) % 2

    @pl.when(own)
    def _():
        move(sems, (here.at[pl.ds(begin, out.shape[0])], out))

    @pl.when(jnp.logical_not(own))
    def _():
        move(sems, (came, out))


NT = (((1,), (1,)), ((), ()))


def absorb_chunk(query, keys, values, biases, state):
    scale = LOG2E / math.sqrt(HD)
    scores = [lax.dot_general(query, k, NT, preferred_element_type=jnp.float32) for k in keys]
    top = None
    for s, b in zip(scores, biases):
        t = jnp.max(s, axis=1, keepdims=True) * scale + b
        top = t if top is None else jnp.maximum(top, t)
    if state is not None:
        old_top, old_sum, old_acc = state
        top = jnp.maximum(old_top, top)
    total, acc = None, None
    for s, b, v in zip(scores, biases, values):
        p = jnp.exp2(s * scale - (top - b))
        part = jnp.sum(p, axis=1, keepdims=True)
        total = part if total is None else total + part
        o = jnp.dot(p.astype(jnp.bfloat16), v, preferred_element_type=jnp.float32)
        acc = o if acc is None else acc + o
    if state is not None:
        factor = jnp.exp2(old_top - top)
        total = total + old_sum * factor
        acc = acc + old_acc * factor
    return top, total, acc


def store_state(acc_out, stat_out, h, state):
    heads = acc_out.shape[1] // HD
    stat_out[:, h : h + 1] = state[0]
    stat_out[:, heads + h : heads + h + 1] = state[1]
    acc_out[:, h * HD : (h + 1) * HD] = state[2]


def frames_kernel(remote, lists, counts, q, *rest):
    kv = rest[: len(SLOTS)]
    acc_out, stat_out = rest[len(SLOTS) :]
    rows, width = kv[0].shape[0], kv[0].shape[1] // 2
    here = lax.axis_index("frame")
    if remote:
        flags = q[rows : rows + 16, :].astype(jnp.float32)
        lane = lax.broadcasted_iota(jnp.int32, (16, width), 1)
    biases = []
    for bit in SLOTS:
        frame = here ^ bit
        if remote:
            seen = jnp.max(jnp.where(lane == frame, flags, 0.0), keepdims=True)
            biases.append(jnp.where(seen > 0.5, 0.0, -jnp.inf))
        else:
            biases.append(jnp.where(visible(frame, lists, counts), 0.0, -jnp.inf))
    group = 4
    for h in range(width // HD):
        keys = slice(h * HD, (h + 1) * HD)
        values = slice(width + h * HD, width + (h + 1) * HD)
        state = None
        for s in range(0, len(SLOTS), group):
            blocks = kv[s : s + group]
            state = absorb_chunk(
                q[:rows, keys],
                [block[:, keys] for block in blocks],
                [block[:, values] for block in blocks],
                biases[s : s + group],
                state,
            )
        store_state(acc_out, stat_out, h, state)


def style_kernel(last, q, held, swapped, acc_in, stat_in, *outs):
    rows, width = acc_in.shape
    heads = width // HD
    core = lax.axis_index("frame") % 2

    def run(keys, values):
        for h in range(heads):
            cols = slice(h * HD, (h + 1) * HD)
            state = (stat_in[:, h : h + 1], stat_in[:, heads + h : heads + h + 1], acc_in[:, cols])
            state = absorb_chunk(
                q[:rows, cols], [keys[:, cols]], [values[:, cols]], [0.0], state
            )
            if last:
                outs[0][:, cols] = (state[2] / state[1]).astype(jnp.bfloat16)
            else:
                store_state(*outs, h, state)

    pl.when(core == 0)(functools.partial(run, held, swapped))
    pl.when(core == 1)(functools.partial(run, swapped, held))


def project_kernel(bit, own, got, weight, *rest):
    came, out = rest[:-1], rest[-1]
    width, columns = own.shape[1], out.shape[1]
    mine, other = halves(width)
    start = pl.multiple_of((lax.axis_index("head") ^ bit) * columns, HD)
    share = jnp.dot(
        own[...],
        weight[pl.ds(mine, width), pl.ds(start, columns)],
        preferred_element_type=jnp.float32,
    ) + jnp.dot(
        got[...],
        weight[pl.ds(other, width), pl.ds(start, columns)],
        preferred_element_type=jnp.float32,
    )
    for block in came:
        share = share + block[...].astype(jnp.float32)
    out[...] = share.astype(out.dtype)


def base_kernel(own, near, residual, gate, out):
    summed = own[...] + near[...].astype(jnp.float32)
    out[...] = residual[...].astype(jnp.float32) + gate[...] * summed


SMEM = pl.BlockSpec(memory_space=pltpu.SMEM)
VMEM = pl.BlockSpec(memory_space=pltpu.VMEM)
ANY = pl.BlockSpec(memory_space=pl.ANY)


def call(kernel, in_specs, outs, scratch=(), out_spec=VMEM, flops=1):
    shapes = [jax.ShapeDtypeStruct(shape, dtype) for shape, dtype in outs]
    return pl.pallas_call(
        kernel,
        out_shape=shapes,
        in_specs=in_specs,
        out_specs=[out_spec] * len(shapes),
        scratch_shapes=list(scratch),
        compiler_params=pltpu.CompilerParams(vmem_limit_bytes=VMEM_LIMIT),
        cost_estimate=pl.CostEstimate(flops=flops, bytes_accessed=1, transcendentals=0),
    )


def dma(count):
    return pltpu.SemaphoreType.DMA((count,))


def later(block, *after, flops=1):
    return call(
        hold_kernel, [ANY] * (1 + len(after)), [(block.shape, block.dtype)], scratch=[dma(1)], flops=flops
    )(block, *after)[0]


def paired_device(
    queries,
    key_rows,
    value_rows,
    ref_keys,
    ref_values,
    key_lists,
    list_counts,
    owner_index,
    out_weight,
    residual,
    gate_scale,
):
    bf16, f32 = jnp.bfloat16, jnp.float32
    rows, columns = queries.shape
    width = columns // 2
    heads = width // HD
    style = ref_keys.shape[1]
    frames = lax.axis_size("frame")

    even = [(i, i ^ CORE) for i in range(0, frames, 2)]
    odd = [(i ^ CORE, i) for i in range(0, frames, 2)]
    with jax.named_scope("core_style"):
        from_even = lax.ppermute(ref_values, "frame", even)
        from_odd = lax.ppermute(ref_keys, "frame", odd)

    right = (lax.axis_index("frame") // ROW) % 2 == 1

    def half_of(block, flag):
        return jnp.where(flag, block[:, width:], block[:, :width])

    kv_send, kv_keep = [
        jnp.concatenate([half_of(key_rows, flag), half_of(value_rows, flag)], axis=1)
        for flag in (jnp.logical_not(right), right)
    ]
    kv_x = swap(kv_send, "frame", ROW, "x_kv")
    kv_y = swap(kv_keep, "frame", COLUMN, "y_kv")
    kv_xy = swap(kv_x, "frame", COLUMN, "xy_kv")

    near = [kv_keep, kv_x, kv_y, kv_xy]
    near = near + [swap(block, "frame", CORE, f"c_kv_{n}") for n, block in enumerate(near)]
    ready = later(kv_x[:16], kv_x, kv_y, flops=4 * 10**10)
    first = style * 16 // 32
    second = style - first
    parts = [((first, width), bf16), ((second, width), bf16)]
    send_a, send_b, keep = call(
        pick_kernel,
        [SMEM] + [ANY] * 5,
        parts + [((style, width), bf16)],
        scratch=[dma(3)],
    )(owner_index, ref_keys, ref_values, from_even, from_odd, ready)
    send_b = later(send_b, near[4])

    def choose(part, bit, begin, here, came, *after):
        return call(
            functools.partial(choose_kernel, bit, begin),
            [SMEM] + [ANY] * (2 + len(after)),
            [part],
            scratch=[dma(1)],
            flops=1,
        )(owner_index, here, came, *after)[0]

    x_came = [swap(sent, "frame", ROW, f"x_style_{j}") for j, sent in enumerate((send_a, send_b))]
    q_keep, q_send = call(
        query_kernel,
        [SMEM, SMEM, ANY, ANY],
        [((rows, width), bf16), ((rows + 16, width), bf16)],
        scratch=[dma(2)],
    )(key_lists, list_counts, queries, kv_y)
    q_got = swap(q_send, "frame", ROW, "x_q")

    state = [((rows, width), f32), ((rows, HD), f32)]

    def frames_of(remote, q):
        return call(
            functools.partial(frames_kernel, remote),
            [SMEM, SMEM] + [VMEM] * 9,
            state,
            flops=3 * 10**9,
        )(key_lists, list_counts, q, *near)

    chosen = [
        choose(parts[j], ROW, j * first, keep, x_came[j], *after)
        for j, after in enumerate(((kv_x,), (kv_xy, *near[4:],)))
    ]
    y_came = [swap(block, "frame", COLUMN, f"y_style_{j}") for j, block in enumerate(chosen)]

    def finish(j, *after):
        held = choose(parts[j], COLUMN, 0, chosen[j], y_came[j], *after)
        return held, swap(held, "frame", CORE, f"c_style_{j}")

    def style_of(last, j, q, blocks, held_state):
        return call(
            functools.partial(style_kernel, last),
            [VMEM] * 5,
            [((rows, width), bf16)] if last else state,
            flops=10**9,
        )(q, *blocks, *held_state)

    own_state = frames_of(False, q_keep)
    their_state = frames_of(True, q_got)
    seen = own_state[1], their_state[1]
    blocks = finish(0, seen[0])
    own_state = style_of(False, 0, q_keep, blocks, own_state)
    their_state = style_of(False, 0, q_got, blocks, their_state)
    blocks = finish(1, *seen)
    (theirs,) = style_of(True, 1, q_got, blocks, their_state)
    got = swap(theirs, "frame", ROW, "x_back")
    (own,) = style_of(True, 1, q_keep, blocks, own_state)

    def project(bit, dtype, *came):
        return call(
            functools.partial(project_kernel, bit),
            [VMEM] * (3 + len(came)),
            [((rows, columns), dtype)],
        )(own, got, out_weight, *came)[0]

    relay = swap(project(3, bf16), "head", 1, "z_relay")
    near_share = swap(project(1, bf16), "head", 1, "z_near")
    far_share = swap(project(2, bf16, relay), "head", 2, "z_far")
    gate = gate_scale[None, :]
    (base,) = call(
        base_kernel, [VMEM] * 4, [((rows, columns), f32)]
    )(project(0, f32), near_share, residual, gate)
    return (base + gate * far_share.astype(f32)).astype(bf16)


def solution(mesh):
    placed = (
        P("frame", "head"),
        P("frame", "head"),
        P("frame", "head"),
        P("frame", None, "head"),
        P("frame", None, "head"),
        P("frame", None),
        P("frame"),
        P(),
        P("head", None),
        P("frame", "head"),
        P("head"),
    )

    def per_device(*args):
        rows, columns = args[0].shape
        style = args[3].shape[1]
        paired = (
            mesh.shape["frame"] == 8
            and mesh.shape["head"] == 4
            and columns % (2 * HD) == 0
            and columns // HD <= HD
            and rows % 16 == 0
            and style % 256 == 0
        )
        return (paired_device if paired else general_device)(*args)

    return jax.shard_map(
        per_device, mesh=mesh, in_specs=placed, out_specs=P("frame", "head"), check_vma=False
    )
```

```python
import functools
import math

import jax
import jax.numpy as jnp
from jax import lax
from jax.experimental import pallas as pl
from jax.experimental.pallas import tpu as pltpu
from jax.sharding import PartitionSpec as P

HD = 128
REACH = 4
LOG2E = 1.4426950408889634
VMEM_LIMIT = 24 * 1024 * 1024


def broadcast(block, axis, source):
    block = jnp.where(lax.axis_index(axis) == source, block, jnp.zeros_like(block))
    return lax.psum(block, axis)


def from_behind(block, axis, distance):
    devices = range(lax.axis_size(axis))
    route = [(i - distance, i) for i in devices if i - distance in devices]
    return lax.ppermute(block, axis, route)


def absorb(carried, query_heads, key_block, value_block, allowed):
    running_max, running_sum, weighted = carried
    head_count = query_heads.shape[1]
    key_heads = key_block.reshape(key_block.shape[0], head_count, HD)
    value_heads = value_block.reshape(value_block.shape[0], head_count, HD)
    scores = jnp.einsum(
        "qhd,khd->hqk", query_heads, key_heads, preferred_element_type=jnp.float32
    ) * (1.0 / math.sqrt(HD))
    if allowed is not None:
        scores = jnp.where(allowed[None, None, :], scores, -jnp.inf)
    new_max = jnp.maximum(running_max, jnp.max(scores, axis=-1))
    factor = jnp.exp(running_max - new_max)
    weights = jnp.exp(scores - new_max[:, :, None])
    running_sum = running_sum * factor + jnp.sum(weights, axis=-1)
    weighted = weighted * factor.T[:, :, None] + jnp.einsum(
        "hqk,khd->qhd",
        weights.astype(jnp.bfloat16),
        value_heads,
        preferred_element_type=jnp.float32,
    )
    return (new_max, running_sum, weighted)


def frame_block(carried, query_heads, key_block, value_block, begin_row, listed, live_slots):
    frame_of = (begin_row + jnp.arange(key_block.shape[0], dtype=jnp.int32)) // query_heads.shape[0]
    allowed = jnp.any((frame_of[:, None] == listed[None, :]) & live_slots[None, :], axis=1)
    return lax.cond(
        jnp.any(allowed),
        lambda current: absorb(current, query_heads, key_block, value_block, allowed),
        lambda current: current,
        carried,
    )


def general_device(
    queries,
    key_rows,
    value_rows,
    ref_keys,
    ref_values,
    key_lists,
    list_counts,
    owner_index,
    out_weight,
    residual,
    gate_scale,
):
    frame_len = queries.shape[0]
    columns_here = queries.shape[1]
    head_count = columns_here // HD
    query_heads = queries.reshape(frame_len, head_count, HD)
    listed = key_lists[0]
    live_slots = jnp.arange(listed.shape[0], dtype=jnp.int32) < list_counts[0]
    position = lax.axis_index("frame")
    carried = (
        jnp.full((head_count, frame_len), -jnp.inf, jnp.float32),
        jnp.zeros((head_count, frame_len), jnp.float32),
        jnp.zeros((frame_len, head_count, HD), jnp.float32),
    )
    style_keys, style_values = (
        broadcast(ref_keys, "frame", owner_index[0]),
        broadcast(ref_values, "frame", owner_index[0]),
    )
    carried = absorb(carried, query_heads, style_keys[0], style_values[0], None)
    carried = absorb(carried, query_heads, key_rows, value_rows, None)
    for offset in list(range(1, REACH + 1)) + list(range(-REACH, 0)):
        moved_keys, moved_values = from_behind((key_rows, value_rows), "frame", offset)
        carried = frame_block(
            carried,
            query_heads,
            moved_keys,
            moved_values,
            (position - offset) * frame_len,
            listed,
            live_slots,
        )
    running_max, running_sum, weighted = carried
    attended = (
        (weighted / running_sum.T[:, :, None]).astype(jnp.bfloat16).reshape(frame_len, columns_here)
    )
    shares = lax.psum_scatter(
        lax.dot_general(
            out_weight, attended, (((0,), (1,)), ((), ())), preferred_element_type=jnp.float32
        ).astype(jnp.bfloat16),
        "head",
        scatter_dimension=0,
        tiled=True,
    ).astype(jnp.float32)
    return (residual.astype(jnp.float32) + gate_scale[None, :] * shares.T).astype(jnp.bfloat16)


CORE, ROW, COLUMN = 1, 2, 4
SLOTS = (0, 2, 4, 6, 1, 3, 5, 7)


def swap(block, axis, bit, name):
    with jax.named_scope(name):
        return lax.ppermute(block, axis, [(i, i ^ bit) for i in range(lax.axis_size(axis))])


def halves(width):
    x = (lax.axis_index("frame") // ROW) % 2
    mine = pl.multiple_of(x * width, HD)
    other = pl.multiple_of((1 - x) * width, HD)
    return mine, other


def visible(frame, lists, counts):
    seen = frame == lax.axis_index("frame")
    for j in range(lists.shape[1]):
        seen = seen | ((lists[0, j] == frame) & (j < counts[0]))
    return seen


def split_kernel(k, v, keep, send, sems):
    rows, width = keep.shape[0], keep.shape[1] // 2
    mine, other = halves(width)
    left, right = pl.ds(0, width), pl.ds(width, width)
    move(
        sems,
        (k.at[:, pl.ds(other, width)], send.at[:, left]),
        (v.at[:, pl.ds(other, width)], send.at[:, right]),
        (k.at[:, pl.ds(mine, width)], keep.at[:, left]),
        (v.at[:, pl.ds(mine, width)], keep.at[:, right]),
    )


def query_kernel(lists, counts, q, after, keep, send, sems):
    rows, width = keep.shape
    mine, other = halves(width)
    lane = lax.broadcasted_iota(jnp.int32, (16, width), 1)
    flags = jnp.zeros((16, width), jnp.float32)
    for g in range(lax.axis_size("frame")):
        flag = jnp.where(visible(g, lists, counts), 1.0, 0.0)
        flags = jnp.where(lane == g, flag, flags)
    send[rows:, :] = flags.astype(jnp.bfloat16)
    move(
        sems,
        (q.at[:, pl.ds(mine, width)], keep),
        (q.at[:, pl.ds(other, width)], send.at[pl.ds(0, rows)]),
    )


def from_owner(owner, k, v, from_even, from_odd, take):
    core = lax.axis_index("frame") % 2
    owner_core = owner[0] % 2
    for at, here, there in ((0, k, from_odd), (1, v, from_even)):
        pl.when((core == at) & (owner_core == at))(functools.partial(take, here))
        pl.when((core == at) & (owner_core != at))(functools.partial(take, there))


def move(sems, *pairs):
    copies = [pltpu.make_async_copy(src, dst, sems.at[i]) for i, (src, dst) in enumerate(pairs)]
    for copy in copies:
        copy.start()
    for copy in copies:
        copy.wait()


def pick_kernel(owner, k, v, from_even, from_odd, after, send_a, send_b, keep, sems):
    first, width = send_a.shape
    second = send_b.shape[0]
    mine, other = halves(width)

    def take(src):
        move(
            sems,
            (src.at[0, pl.ds(0, first), pl.ds(other, width)], send_a),
            (src.at[0, pl.ds(first, second), pl.ds(other, width)], send_b),
            (src.at[0, :, pl.ds(mine, width)], keep),
        )

    from_owner(owner, k, v, from_even, from_odd, take)


def hold_kernel(block, *rest):
    out, sems = rest[-2:]
    move(sems, (block, out))


def choose_kernel(bit, begin, owner, here, came, *rest):
    out, sems = rest[-2:]
    own = (owner[0] // bit) % 2 == (lax.axis_index("frame") // bit) % 2

    @pl.when(own)
    def _():
        move(sems, (here.at[pl.ds(begin, out.shape[0])], out))

    @pl.when(jnp.logical_not(own))
    def _():
        move(sems, (came, out))


NT = (((1,), (1,)), ((), ()))


def absorb_chunk(query, keys, values, biases, state):
    scale = LOG2E / math.sqrt(HD)
    scores = [lax.dot_general(query, k, NT, preferred_element_type=jnp.float32) for k in keys]
    top = None
    for s, b in zip(scores, biases):
        t = jnp.max(s, axis=1, keepdims=True) * scale + b
        top = t if top is None else jnp.maximum(top, t)
    if state is not None:
        old_top, old_sum, old_acc = state
        top = jnp.maximum(old_top, top)
    total, acc = None, None
    for s, b, v in zip(scores, biases, values):
        p = jnp.exp2(s * scale - (top - b))
        part = jnp.sum(p, axis=1, keepdims=True)
        total = part if total is None else total + part
        o = jnp.dot(p.astype(jnp.bfloat16), v, preferred_element_type=jnp.float32)
        acc = o if acc is None else acc + o
    if state is not None:
        factor = jnp.exp2(old_top - top)
        total = total + old_sum * factor
        acc = acc + old_acc * factor
    return top, total, acc


def store_state(acc_out, stat_out, h, state):
    heads = acc_out.shape[1] // HD
    stat_out[:, h : h + 1] = state[0]
    stat_out[:, heads + h : heads + h + 1] = state[1]
    acc_out[:, h * HD : (h + 1) * HD] = state[2]


def frames_kernel(remote, lists, counts, q, *rest):
    kv = rest[: len(SLOTS)]
    acc_out, stat_out = rest[len(SLOTS) :]
    rows, width = kv[0].shape[0], kv[0].shape[1] // 2
    here = lax.axis_index("frame")
    if remote:
        flags = q[rows : rows + 16, :].astype(jnp.float32)
        lane = lax.broadcasted_iota(jnp.int32, (16, width), 1)
    biases = []
    for bit in SLOTS:
        frame = here ^ bit
        if remote:
            seen = jnp.max(jnp.where(lane == frame, flags, 0.0), keepdims=True)
            biases.append(jnp.where(seen > 0.5, 0.0, -jnp.inf))
        else:
            biases.append(jnp.where(visible(frame, lists, counts), 0.0, -jnp.inf))
    group = 4
    for h in range(width // HD):
        keys = slice(h * HD, (h + 1) * HD)
        values = slice(width + h * HD, width + (h + 1) * HD)
        state = None
        for s in range(0, len(SLOTS), group):
            blocks = kv[s : s + group]
            state = absorb_chunk(
                q[:rows, keys],
                [block[:, keys] for block in blocks],
                [block[:, values] for block in blocks],
                biases[s : s + group],
                state,
            )
        store_state(acc_out, stat_out, h, state)


def style_kernel(last, q, held, swapped, acc_in, stat_in, *outs):
    rows, width = acc_in.shape
    heads = width // HD
    core = lax.axis_index("frame") % 2

    def run(keys, values):
        for h in range(heads):
            cols = slice(h * HD, (h + 1) * HD)
            state = (stat_in[:, h : h + 1], stat_in[:, heads + h : heads + h + 1], acc_in[:, cols])
            state = absorb_chunk(
                q[:rows, cols], [keys[:, cols]], [values[:, cols]], [0.0], state
            )
            if last:
                outs[0][:, cols] = (state[2] / state[1]).astype(jnp.bfloat16)
            else:
                store_state(*outs, h, state)

    pl.when(core == 0)(functools.partial(run, held, swapped))
    pl.when(core == 1)(functools.partial(run, swapped, held))


def project_kernel(bit, own, got, weight, *rest):
    came, out = rest[:-1], rest[-1]
    width, columns = own.shape[1], out.shape[1]
    mine, other = halves(width)
    start = pl.multiple_of((lax.axis_index("head") ^ bit) * columns, HD)
    share = jnp.dot(
        own[...],
        weight[pl.ds(mine, width), pl.ds(start, columns)],
        preferred_element_type=jnp.float32,
    ) + jnp.dot(
        got[...],
        weight[pl.ds(other, width), pl.ds(start, columns)],
        preferred_element_type=jnp.float32,
    )
    for block in came:
        share = share + block[...].astype(jnp.float32)
    out[...] = share.astype(out.dtype)


def base_kernel(own, near, residual, gate, out):
    summed = own[...] + near[...].astype(jnp.float32)
    out[...] = residual[...].astype(jnp.float32) + gate[...] * summed


SMEM = pl.BlockSpec(memory_space=pltpu.SMEM)
VMEM = pl.BlockSpec(memory_space=pltpu.VMEM)
ANY = pl.BlockSpec(memory_space=pl.ANY)


def call(kernel, in_specs, outs, scratch=(), out_spec=VMEM, flops=1):
    shapes = [jax.ShapeDtypeStruct(shape, dtype) for shape, dtype in outs]
    return pl.pallas_call(
        kernel,
        out_shape=shapes,
        in_specs=in_specs,
        out_specs=[out_spec] * len(shapes),
        scratch_shapes=list(scratch),
        compiler_params=pltpu.CompilerParams(vmem_limit_bytes=VMEM_LIMIT),
        cost_estimate=pl.CostEstimate(flops=flops, bytes_accessed=1, transcendentals=0),
    )


def dma(count):
    return pltpu.SemaphoreType.DMA((count,))


def later(block, *after, flops=1):
    return call(
        hold_kernel, [ANY] * (1 + len(after)), [(block.shape, block.dtype)], scratch=[dma(1)], flops=flops
    )(block, *after)[0]


def paired_device(
    queries,
    key_rows,
    value_rows,
    ref_keys,
    ref_values,
    key_lists,
    list_counts,
    owner_index,
    out_weight,
    residual,
    gate_scale,
):
    bf16, f32 = jnp.bfloat16, jnp.float32
    rows, columns = queries.shape
    width = columns // 2
    heads = width // HD
    style = ref_keys.shape[1]
    frames = lax.axis_size("frame")

    even = [(i, i ^ CORE) for i in range(0, frames, 2)]
    odd = [(i ^ CORE, i) for i in range(0, frames, 2)]
    with jax.named_scope("core_style"):
        from_even = lax.ppermute(ref_values, "frame", even)
        from_odd = lax.ppermute(ref_keys, "frame", odd)

    right = (lax.axis_index("frame") // ROW) % 2 == 1

    def half_of(block, flag):
        return jnp.where(flag, block[:, width:], block[:, :width])

    kv_send, kv_keep = [
        jnp.concatenate([half_of(key_rows, flag), half_of(value_rows, flag)], axis=1)
        for flag in (jnp.logical_not(right), right)
    ]
    kv_x = swap(kv_send, "frame", ROW, "x_kv")
    kv_y = swap(kv_keep, "frame", COLUMN, "y_kv")
    kv_xy = swap(kv_x, "frame", COLUMN, "xy_kv")

    near = [kv_keep, kv_x, kv_y, kv_xy]
    near = near + [swap(block, "frame", CORE, f"c_kv_{n}") for n, block in enumerate(near)]
    ready = later(kv_x[:16], kv_x, kv_y, flops=4 * 10**10)
    first = style * 16 // 32
    second = style - first
    parts = [((first, width), bf16), ((second, width), bf16)]
    send_a, send_b, keep = call(
        pick_kernel,
        [SMEM] + [ANY] * 5,
        parts + [((style, width), bf16)],
        scratch=[dma(3)],
    )(owner_index, ref_keys, ref_values, from_even, from_odd, ready)
    send_b = later(send_b, near[4])

    def choose(part, bit, begin, here, came, *after):
        return call(
            functools.partial(choose_kernel, bit, begin),
            [SMEM] + [ANY] * (2 + len(after)),
            [part],
            scratch=[dma(1)],
            flops=1,
        )(owner_index, here, came, *after)[0]

    x_came = [swap(sent, "frame", ROW, f"x_style_{j}") for j, sent in enumerate((send_a, send_b))]
    q_keep, q_send = call(
        query_kernel,
        [SMEM, SMEM, ANY, ANY],
        [((rows, width), bf16), ((rows + 16, width), bf16)],
        scratch=[dma(2)],
    )(key_lists, list_counts, queries, kv_y)
    q_got = swap(q_send, "frame", ROW, "x_q")

    state = [((rows, width), f32), ((rows, HD), f32)]

    def frames_of(remote, q):
        return call(
            functools.partial(frames_kernel, remote),
            [SMEM, SMEM] + [VMEM] * 9,
            state,
            flops=3 * 10**9,
        )(key_lists, list_counts, q, *near)

    chosen = [
        choose(parts[j], ROW, j * first, keep, x_came[j], *after)
        for j, after in enumerate(((kv_x, kv_y), (kv_xy, *near[4:])))
    ]
    y_came = [swap(block, "frame", COLUMN, f"y_style_{j}") for j, block in enumerate(chosen)]

    def finish(j, *after):
        held = choose(parts[j], COLUMN, 0, chosen[j], y_came[j], *after)
        return held, swap(held, "frame", CORE, f"c_style_{j}")

    def style_of(last, j, q, blocks, held_state):
        return call(
            functools.partial(style_kernel, last),
            [VMEM] * 5,
            [((rows, width), bf16)] if last else state,
            flops=10**9,
        )(q, *blocks, *held_state)

    own_state = frames_of(False, q_keep)
    their_state = frames_of(True, q_got)
    seen = own_state[1], their_state[1]
    blocks = finish(0, seen[0])
    own_state = style_of(False, 0, q_keep, blocks, own_state)
    their_state = style_of(False, 0, q_got, blocks, their_state)
    blocks = finish(1, *seen)
    (theirs,) = style_of(True, 1, q_got, blocks, their_state)
    got = swap(theirs, "frame", ROW, "x_back")
    (own,) = style_of(True, 1, q_keep, blocks, own_state)

    def project(bit, dtype, *came):
        return call(
            functools.partial(project_kernel, bit),
            [VMEM] * (3 + len(came)),
            [((rows, columns), dtype)],
        )(own, got, out_weight, *came)[0]

    relay = swap(project(3, bf16), "head", 1, "z_relay")
    near_share = swap(project(1, bf16), "head", 1, "z_near")
    far_share = swap(project(2, bf16, relay), "head", 2, "z_far")
    gate = gate_scale[None, :]
    (base,) = call(
        base_kernel, [VMEM] * 4, [((rows, columns), f32)]
    )(project(0, f32), near_share, residual, gate)
    return (base + gate * far_share.astype(f32)).astype(bf16)


def solution(mesh):
    placed = (
        P("frame", "head"),
        P("frame", "head"),
        P("frame", "head"),
        P("frame", None, "head"),
        P("frame", None, "head"),
        P("frame", None),
        P("frame"),
        P(),
        P("head", None),
        P("frame", "head"),
        P("head"),
    )

    def per_device(*args):
        rows, columns = args[0].shape
        style = args[3].shape[1]
        paired = (
            mesh.shape["frame"] == 8
            and mesh.shape["head"] == 4
            and columns % (2 * HD) == 0
            and columns // HD <= HD
            and rows % 16 == 0
            and style % 256 == 0
        )
        return (paired_device if paired else general_device)(*args)

    return jax.shard_map(
        per_device, mesh=mesh, in_specs=placed, out_specs=P("frame", "head"), check_vma=False
    )
```
